32 devices in a mesh: dp: 8 (over z, y), fsdp: 4 (over x, core).
Axes of the slice: x: 2, y: 2, z: 4, core: 2. Of those that a mesh axis runs over, the one named last changes fastest.
Arguments:
- hidden_in: bfloat16 [2, 32, 512, 1024], P(None, ('dp', 'fsdp')), may hold values from -6 to 6
- cotangent: bfloat16 [2, 32, 512, 1024], P(None, ('dp', 'fsdp')), may hold values from -6 to 6
- seg_lengths: int32 [2, 32, 4], P(None, ('dp', 'fsdp')), may hold values from 1 to 400, as said below
- retrieved: int32 [2, 32, 4, 5], P(None, ('dp', 'fsdp')), may hold values from 0 to 255, as said below
- encoder_states: bfloat16 [256, 64, 1024], P(('dp', 'fsdp')), may hold values from -6 to 6
- master_weights: float32 [1024, 16384], P(None, ('dp', 'fsdp')), as said below
- first_moment: float32 [1024, 16384], P(None, ('dp', 'fsdp')), may hold values from -40 to 40
- second_moment: float32 [1024, 16384], P(None, ('dp', 'fsdp')), may hold values from 2.94912 to 11.79648
- slot_block: int32 [128], replicated, may hold values from 0 to 127, as said below
- bases: float32 [10, 1024, 1024], replicated, may hold values from -0.1875 to 0.1875
- vector_params: float32 [17, 1024], P(None, ('dp', 'fsdp')), as said below
- vector_first: float32 [17, 1024], P(None, ('dp', 'fsdp')), may hold values from -40 to 40
- vector_second: float32 [17, 1024], P(None, ('dp', 'fsdp')), may hold values from 2.94912 to 11.79648
Outputs:
- block_out: bfloat16 [2, 32, 512, 1024], P(None, ('dp', 'fsdp'))
- hidden_grad: bfloat16 [2, 32, 512, 1024], P(None, ('dp', 'fsdp'))
- encoder_grad: bfloat16 [256, 64, 1024], P(('dp', 'fsdp'))
- new_first: float32 [1024, 16384], P(None, ('dp', 'fsdp'))
- new_second: float32 [1024, 16384], P(None, ('dp', 'fsdp'))
- new_master: float32 [1024, 16384], P(None, ('dp', 'fsdp'))
- vector_first_new: float32 [17, 1024], P(None, ('dp', 'fsdp'))
- vector_second_new: float32 [17, 1024], P(None, ('dp', 'fsdp'))
- vector_new: float32 [17, 1024], P(None, ('dp', 'fsdp'))
- vector_grad: float32 [17, 1024], P(None, ('dp', 'fsdp'))
The draws below stay inside these ranges and needn't reach their ends.
Inputs may be any that keep to these rules, and one draw needn't show every extreme that they name: `seg_lengths`: each row's 4 lengths sum to 512; the first row holds a segment of 400. `retrieved`: A row's passages lie among the 32 passages of the rows' index of dp, in order of devices. `slot_block`: A permutation of the 128 blocks. `master_weights`: entries of order of the weights' spread. `vector_params`: gains near 1, biases of order a third.
All inputs are finite; a program needn't handle non-finite values.
Results may differ from the reference program's by a relative error of at most 0.022.
The reference program's roundings to bfloat16 on the way count: a program that leaves them out, or rounds other values in their place, can miss the bound.
Values may be sent and summed in bfloat16 or wider, within the bound.
No kernel may reach another device: no remote copies, remote signals or barrier semaphores. Data moves between devices by JAX's collectives and lax.ppermute only.
A program may use at most 576 MiB of HBM per device.

```python
import math
import jax
import jax.numpy as jnp
from jax import lax

D = 1024
HEADS = 16
HD = 64
FF = 4096
ENC_LEN = 64
NRET = 5
ROW = 512
SEGS = 4
LONG = 400
SHORT = 100
MICRO = 2
ROWS_DEV = 1
PASS_DEV = 8
BLK = 128
STEP = 5
NMAT = 10
ROWS = 32
POOL = 256
PASS_GRP = 32
COLS = 16384
NVEC = 17


def slot_order(key):
    return jax.random.permutation(jax.random.fold_in(key, 11), COLS // BLK).astype(jnp.int32)


def draw_slot_block(key, part):
    return slot_order(key)


def draw_master_weights(key, part):
    order = slot_order(key)
    column = jnp.arange(COLS, dtype=jnp.int32)
    natural = jnp.repeat(order, BLK) * BLK + column % BLK
    base = D ** (-0.5)
    scale = jnp.full((COLS,), base, jnp.float32)
    scale = jnp.where((natural >= 3 * D) & (natural < 4 * D), base * (SHORT / 4.0) ** 0.5, scale)
    scale = jnp.where((natural >= 7 * D) & (natural < 8 * D), base * (NRET * ENC_LEN / 4.0) ** 0.5, scale)
    scale = jnp.where(natural >= 8 * D + FF, FF ** (-0.5), scale)
    raw = jax.random.normal(jax.random.fold_in(key, 12), (D, COLS), jnp.float32)
    return raw * scale[None, :]


def draw_vector_params(key, part):
    raw = jax.random.normal(jax.random.fold_in(key, 13), (NVEC, D), jnp.float32)
    row = jnp.arange(NVEC)
    is_gain = (row == 3) | (row == 8) | (row == 11)
    return jnp.where(is_gain[:, None], 1.0 + 0.1 * raw, 0.3 * raw)


def draw_seg_lengths(key, part):
    nrows = MICRO * ROWS
    key_one = jax.random.fold_in(key, 21)
    key_two = jax.random.fold_in(key, 22)
    key_three = jax.random.fold_in(key, 23)
    is_long = jax.random.randint(key_one, (nrows,), 0, 4) == 0
    is_long = is_long.at[0].set(True)
    short = jax.random.randint(key_two, (nrows, SEGS - 1), SHORT // 2, SHORT + 1)
    short_row = jnp.concatenate([short, ROW - jnp.sum(short, axis=1, keepdims=True)], axis=1)
    piece = (ROW - LONG) // (SEGS - 1)
    middle = jax.random.randint(key_three, (nrows, SEGS - 2), 1, piece + 1)
    long_last = ROW - LONG - jnp.sum(middle, axis=1, keepdims=True)
    long_row = jnp.concatenate([jnp.full((nrows, 1), LONG, jnp.int32), middle, long_last], axis=1)
    chosen = jnp.where(is_long[:, None], long_row, short_row)
    return chosen.reshape(MICRO, ROWS, SEGS).astype(jnp.int32)


def draw_retrieved(key, part):
    local = jax.random.randint(jax.random.fold_in(key, 31), (MICRO, ROWS, SEGS, NRET), 0, PASS_GRP)
    local = local.at[:, :, 0, 0].set(0)
    local = local.at[:, :, 0, 1].set(PASS_GRP - 1)
    row = jnp.arange(ROWS, dtype=jnp.int32)
    group = row // ROWS_DEV // (PASS_GRP // PASS_DEV)
    return (local + group[None, :, None, None] * PASS_GRP).astype(jnp.int32)


def block_scale(stream_key, shape, shards, smallest, high):
    loudness, own = 1.0, jax.random.fold_in(stream_key, 6)
    for dim, blocks in shards:
        draws = jnp.exp(jax.random.uniform(jax.random.fold_in(own, dim), (blocks,), jnp.float32, smallest / len(shards), high / len(shards)))
        loudness = loudness * jnp.repeat(draws, shape[dim] // blocks).reshape([-1 if axis == dim else 1 for axis in range(len(shape))])
    return loudness


def noise(key, shape, spread, most, cuts=(), kind=jnp.bfloat16):
    entries = spread * jax.random.normal(key, shape, jnp.float32)
    if cuts:
        entries = entries * block_scale(key, shape, cuts, -0.22, 0.18)
    return jnp.clip(entries, -most, most).astype(kind)


def setup_inputs(seed: int = 0) -> dict:
    streams_of = jax.random.split(jax.random.key(seed), 14)
    hidden_in = noise(streams_of[0], (MICRO, ROWS, ROW, D), 1.0, 6.0, ((1, 32),))
    cotangent = noise(streams_of[1], (MICRO, ROWS, ROW, D), 1.0, 6.0, ((1, 32),))
    seg_lengths = draw_seg_lengths(jax.random.fold_in(streams_of[13], 71), 0)
    retrieved = draw_retrieved(jax.random.fold_in(streams_of[13], 71), 0)
    encoder_states = noise(streams_of[4], (POOL, ENC_LEN, D), 1.0, 6.0, ((0, 32),))
    master_weights = draw_master_weights(jax.random.fold_in(streams_of[13], 71), 0)
    first_moment = noise(streams_of[6], (D, COLS), (0.037 * (MICRO * ROWS * ROW) ** 0.5), 40.0, ((1, 32),), jnp.float32)
    second_moment = jnp.clip(jnp.exp(math.log(11.79648) - 1.3862944 * jax.random.uniform(streams_of[7], (D, COLS), jnp.float32) ** block_scale(streams_of[7], (D, COLS), ((1, 32),), -0.2, 0.2)), 2.94912, 11.79648)
    slot_block = draw_slot_block(jax.random.fold_in(streams_of[13], 71), 0)
    bases = noise(streams_of[9], (NMAT, D, D), D ** -0.5, 0.1875, (), jnp.float32)
    vector_params = draw_vector_params(jax.random.fold_in(streams_of[13], 71), 0)
    vector_first = noise(streams_of[11], (NVEC, D), (0.037 * (MICRO * ROWS * ROW) ** 0.5), 40.0, ((1, 32),), jnp.float32)
    vector_second = jnp.clip(jnp.exp(math.log(11.79648) - 1.3862944 * jax.random.uniform(streams_of[12], (NVEC, D), jnp.float32) ** block_scale(streams_of[12], (NVEC, D), ((1, 32),), -0.2, 0.2)), 2.94912, 11.79648)
    return dict(hidden_in=hidden_in, cotangent=cotangent, seg_lengths=seg_lengths, retrieved=retrieved, encoder_states=encoder_states, master_weights=master_weights, first_moment=first_moment, second_moment=second_moment, slot_block=slot_block, bases=bases, vector_params=vector_params, vector_first=vector_first, vector_second=vector_second)


@jax.custom_vjp
def low(v):
    return lax.optimization_barrier(v.astype(jnp.bfloat16)).astype(jnp.float32)

@jax.custom_vjp
def low_back(v):
    return v

def low_keep(v):
    return (low(v), None)

def low_pass(kept, grad):
    return (grad,)

def back_keep(v):
    return (v, None)

def back_low(kept, grad):
    return (low(grad),)
low.defvjp(low_keep, low_pass)
low_back.defvjp(back_keep, back_low)
HIGH = lax.Precision.HIGHEST
eps_norm = 1e-05
beta_one = 0.9
beta_two = 0.999
adam_eps = 1e-08
rate_mat = 0.03
rate_vec = 0.25
decay = 0.01
neg_big = -1e+30

def matmul(a, b):
    return jnp.dot(a, b, precision=HIGH, preferred_element_type=jnp.float32)

def layer_norm(resid, gain, shift):
    mean_row = lax.optimization_barrier(jnp.mean(resid, axis=-1, keepdims=True))
    centred = resid - mean_row
    inv = lax.rsqrt(lax.optimization_barrier(jnp.mean(centred * centred, axis=-1, keepdims=True)) + eps_norm)
    return centred * inv * gain + shift

def attend(query, keys, values, allowed):
    rows = query.shape[0]
    width = keys.shape[0]
    q_heads = query.reshape(rows, HEADS, HD)
    k_heads = keys.reshape(width, HEADS, HD)
    v_heads = values.reshape(width, HEADS, HD)
    scores = jnp.einsum('thd,shd->hts', q_heads, k_heads, precision=HIGH) * HD ** (-0.5)
    scores = low_back(scores)
    scores = jnp.where(allowed[None], scores, neg_big)
    top = lax.optimization_barrier(jnp.max(scores, axis=-1, keepdims=True))
    expo = jnp.exp(scores - top)
    probs = expo / lax.optimization_barrier(jnp.sum(expo, axis=-1, keepdims=True))
    out = jnp.einsum('hts,shd->thd', low(probs), v_heads, precision=HIGH)
    return low_back(low(out.reshape(rows, HEADS * HD)))

def layer(params, x_row, enc_row, allowed_self, allowed_cross):
    w_q, w_k, w_v, w_o, c_q, c_k, c_v, c_o, w_up, w_downt, vecs = params
    b_up = vecs[13:].reshape(-1)
    query = low_back(low(matmul(x_row, w_q) + vecs[0]))
    keys = low_back(low(matmul(x_row, w_k)))
    values = low_back(low(matmul(x_row, w_v) + vecs[1]))
    attn_self = attend(query, keys, values, allowed_self)
    branch = low_back(matmul(attn_self, w_o) + vecs[2])
    hid_one = layer_norm(x_row + branch, vecs[3], vecs[4])
    hid_low = low(hid_one)
    c_query = low_back(low(matmul(hid_low, c_q) + vecs[5]))
    c_keys = low_back(low(matmul(enc_row, c_k)))
    c_values = low_back(low(matmul(enc_row, c_v) + vecs[6]))
    attn_cross = attend(c_query, c_keys, c_values, allowed_cross)
    branch_two = low_back(matmul(attn_cross, c_o) + vecs[7])
    hid_two = layer_norm(hid_one + branch_two, vecs[8], vecs[9])
    upper = low_back(matmul(low(hid_two), w_up) + b_up)
    act = low(jax.nn.gelu(upper, approximate=False))
    branch_three = low_back(matmul(act, w_downt.T) + vecs[10])
    return layer_norm(hid_two + branch_three, vecs[11], vecs[12])

def reference(hidden_in, cotangent, seg_lengths, retrieved, encoder_states, master_weights, first_moment, second_moment, slot_block, bases, vector_params, vector_first, vector_second):
    nblk = COLS // BLK
    inverse = jnp.zeros((nblk,), jnp.int32).at[slot_block].set(jnp.arange(nblk, dtype=jnp.int32))
    natural = jnp.take(master_weights.reshape(D, nblk, BLK), inverse, axis=1).reshape(D, COLS)
    weights = low(natural)
    mats = [weights[:, j * D:(j + 1) * D] for j in range(8)]
    mats = mats + [weights[:, 8 * D:8 * D + FF], weights[:, 8 * D + FF:]]
    vecs = low(vector_params)
    params = tuple(mats) + (vecs,)
    rows_x = hidden_in.reshape(MICRO * ROWS, ROW, D).astype(jnp.float32)
    rows_c = cotangent.reshape(MICRO * ROWS, ROW, D).astype(jnp.float32)
    lens = seg_lengths.reshape(MICRO * ROWS, SEGS)
    rets = retrieved.reshape(MICRO * ROWS, SEGS * NRET)
    enc_all = encoder_states.astype(jnp.float32)
    position = jnp.arange(ROW, dtype=jnp.int32)
    key_seg = jnp.arange(SEGS * NRET * ENC_LEN, dtype=jnp.int32) // (NRET * ENC_LEN)

    def one_row(carry, item):
        grads, enc_grad = carry
        x_row, c_row, len_row, ret_row = item
        ends = jnp.cumsum(len_row)
        qseg = lax.optimization_barrier(jnp.sum((position[:, None] >= ends[None, :-1]).astype(jnp.int32), axis=1))
        allowed_self = (qseg[:, None] == qseg[None, :]) & (position[:, None] >= position[None, :])
        allowed_cross = qseg[:, None] == key_seg[None, :]
        enc_row = jnp.take(enc_all, ret_row, axis=0).reshape(SEGS * NRET * ENC_LEN, D)
        out, pull = jax.vjp(lambda pp, xx, ee: layer(pp, xx, ee, allowed_self, allowed_cross), params, x_row, enc_row)
        g_params, g_x, g_enc = pull(c_row)
        grads = jax.tree.map(lambda a, b: a + b, grads, g_params)
        enc_grad = enc_grad.at[ret_row].add(g_enc.reshape(SEGS * NRET, ENC_LEN, D))
        return ((grads, enc_grad), (out.astype(jnp.bfloat16), g_x.astype(jnp.bfloat16)))
    start = (jax.tree.map(jnp.zeros_like, params), jnp.zeros((POOL, ENC_LEN, D), jnp.float32))
    (grads, enc_grad), (outs, gxs) = lax.scan(one_row, start, (rows_x, rows_c, lens, rets))
    grad_nat = jnp.concatenate(list(grads[:10]), axis=1)
    grad_slot = jnp.take(grad_nat.reshape(D, nblk, BLK), slot_block, axis=1)
    bounds = jnp.array([D, 2 * D, 3 * D, 4 * D, 5 * D, 6 * D, 7 * D, 8 * D, 8 * D + FF], jnp.int32)
    which = lax.optimization_barrier(jnp.sum((slot_block[:, None] * BLK >= bounds[None, :]).astype(jnp.int32), axis=1))
    corr_one = 1.0 - beta_one ** STEP
    corr_two = 1.0 - beta_two ** STEP

    def owner_step(item):
        grad_blk, first_blk, second_blk, master_blk, mat = item
        basis = bases[mat]
        turned = jnp.dot(basis.T, grad_blk, precision=HIGH, preferred_element_type=jnp.float32)
        first_new = beta_one * first_blk + (1.0 - beta_one) * turned
        second_new = beta_two * second_blk + (1.0 - beta_two) * turned * turned
        step = first_new / corr_one / (jnp.sqrt(second_new / corr_two) + adam_eps)
        back = jnp.dot(basis, step, precision=HIGH, preferred_element_type=jnp.float32)
        return (first_new, second_new, master_blk - rate_mat * (back + decay * master_blk))

    def blocks_of(arr):
        return jnp.transpose(arr.reshape(D, nblk, BLK), (1, 0, 2))

    def unblock(arr):
        return jnp.transpose(arr, (1, 0, 2)).reshape(D, COLS)
    f_new, s_new, m_new = lax.map(owner_step, (jnp.transpose(grad_slot, (1, 0, 2)), blocks_of(first_moment), blocks_of(second_moment), blocks_of(master_weights), which))
    grad_vec = grads[10]
    vf_new = beta_one * vector_first + (1.0 - beta_one) * grad_vec
    vs_new = beta_two * vector_second + (1.0 - beta_two) * grad_vec * grad_vec
    vec_new = vector_params - rate_vec * (vf_new / corr_one) / (jnp.sqrt(vs_new / corr_two) + adam_eps)
    block_out = outs.reshape(MICRO, ROWS, ROW, D)
    hidden_grad = gxs.reshape(MICRO, ROWS, ROW, D)
    return (block_out, hidden_grad, enc_grad.astype(jnp.bfloat16), unblock(f_new), unblock(s_new), unblock(m_new), vf_new, vs_new, vec_new, grad_vec)
```

```python
import functools

import jax
import jax.numpy as jnp
from jax import lax
from jax.experimental import pallas as pl
from jax.experimental.pallas import tpu as pltpu
from jax.sharding import PartitionSpec as P

HD = 64
STEP = 5
NH = 4
TR = 64
AXES = ("dp", "fsdp")
HI = 8

bf = jnp.bfloat16
f32 = jnp.float32
eps_norm = 1e-05
beta_one = 0.9
beta_two = 0.999
adam_eps = 1e-08
rate_mat = 0.03
rate_vec = 0.25
decay = 0.01

def nt(a,b): return lax.dot_general(a,b,(((1,),(1,)),((),())),preferred_element_type=f32)
def nn(a,b): return lax.dot_general(a,b,(((1,),(0,)),((),())),preferred_element_type=f32)
def tn(a,b): return lax.dot_general(a,b,(((0,),(0,)),((),())),preferred_element_type=f32)

def spread(tile, scale):
    lane_head = lax.broadcasted_iota(jnp.int32, tile.shape, 1) // HD
    tile = tile * jnp.asarray(scale, tile.dtype) if scale != 1.0 else tile
    zero = jnp.zeros_like(tile)
    return jnp.concatenate([jnp.where(lane_head == h, tile, zero) for h in range(NH)], axis=0)

def collect(big):
    tr = big.shape[0] // NH
    lane_head = lax.broadcasted_iota(jnp.int32, (tr, big.shape[1]), 1) // HD
    out = big[:tr]
    for h in range(1, NH):
        out = jnp.where(lane_head == h, big[h*tr:(h+1)*tr], out)
    return out

def softmax_t(scores):
    top = jnp.max(scores, axis=0, keepdims=True)
    expo = jnp.exp(scores - top)
    total = jnp.sum(expo, axis=0, keepdims=True)
    return expo * (1.0 / total)

def seg_of(pos, lens_ref, row, segs):
    end = lens_ref[row, 0]
    seg = (pos >= end).astype(jnp.int32)
    for i in range(1, segs - 1):
        end = end + lens_ref[row, i]
        seg = seg + (pos >= end).astype(jnp.int32)
    return seg

def build_bias(bias_ref, lens_ref, row, segs):
    n = bias_ref.shape[0]
    key = lax.broadcasted_iota(jnp.int32, (n, n), 0)
    que = lax.broadcasted_iota(jnp.int32, (n, n), 1)
    kseg = seg_of(lax.broadcasted_iota(jnp.int32, (n, 1), 0), lens_ref, row, segs)
    qseg = seg_of(lax.broadcasted_iota(jnp.int32, (1, n), 1), lens_ref, row, segs)
    ok = (kseg == qseg) & (key <= que)
    bias_ref[...] = jnp.where(ok, 0.0, -1e30)

def bias_tile(bias_ref, first, width, tr):
    piece = bias_ref[:width, first:first+tr]
    return jnp.concatenate([piece]*NH, axis=1)

def self_fwd_kernel(segs, lens_ref, q_ref, k_ref, v_ref, o_ref, bias_ref):
    row = pl.program_id(0)
    n = q_ref.shape[0]
    @pl.when(pl.program_id(1) == 0)
    def _():
        build_bias(bias_ref, lens_ref, row, segs)
    for t in range(n // TR):
        w = (t + 1) * TR
        big = spread(q_ref[t*TR:(t+1)*TR, :], HD ** -0.5)
        s = nt(k_ref[:w, :], big) + bias_tile(bias_ref, t*TR, w, TR)
        p = softmax_t(s).astype(bf)
        o_ref[t*TR:(t+1)*TR, :] = collect(tn(p, v_ref[:w, :])).astype(bf)

def self_fwd(lens, qkv, rows):
    tok, width3 = qkv.shape
    width = width3 // 3
    n = tok // rows
    lanes = NH * HD
    nb = width // lanes
    spec = lambda off: pl.BlockSpec((n, lanes), lambda r, h, *_: (r, off*nb + h))
    return pl.pallas_call(
        functools.partial(self_fwd_kernel, lens.shape[1]),
        grid_spec=pltpu.PrefetchScalarGridSpec(num_scalar_prefetch=1, grid=(rows, nb),
            in_specs=[spec(0), spec(1), spec(2)], out_specs=spec(0),
            scratch_shapes=[pltpu.VMEM((n, n), f32)]),
        out_shape=jax.ShapeDtypeStruct((tok, width), bf),
        compiler_params=pltpu.CompilerParams(vmem_limit_bytes=48<<20),
        cost_estimate=pl.CostEstimate(flops=2*tok*n*width, bytes_accessed=8*tok*width, transcendentals=tok*n*width//HD//2),
    )(lens, qkv, qkv, qkv)

def self_bwd_kernel(segs, lens_ref, q_ref, k_ref, v_ref, g_ref, out_ref, bias_ref, dq_ref, ak_ref, av_ref):
    row = pl.program_id(0)
    part = pl.program_id(2)

    @pl.when((pl.program_id(1) == 0) & (part == 0))
    def _():
        build_bias(bias_ref, lens_ref, row, segs)

    @pl.when(part == 0)
    def _():
        self_bwd_body(q_ref, k_ref, v_ref, g_ref, bias_ref, dq_ref, ak_ref, av_ref)
        out_ref[...] = dq_ref[...]

    @pl.when(part == 1)
    def _():
        out_ref[...] = ak_ref[...].astype(bf)

    @pl.when(part == 2)
    def _():
        out_ref[...] = av_ref[...].astype(bf)

def self_bwd_body(q_ref, k_ref, v_ref, g_ref, bias_ref, dq_ref, ak_ref, av_ref):
    n = q_ref.shape[0]
    for t in reversed(range(n // TR)):
        w = (t + 1) * TR
        big = spread(q_ref[t*TR:(t+1)*TR, :], HD ** -0.5)
        gbig = spread(g_ref[t*TR:(t+1)*TR, :], 1.0)
        k = k_ref[:w, :]
        p = softmax_t(nt(k, big) + bias_tile(bias_ref, t*TR, w, TR))
        u = p * nt(v_ref[:w, :], gbig)
        ds = (u - p * jnp.sum(u, axis=0, keepdims=True)).astype(bf)
        av = nn(p.astype(bf), gbig)
        ak = nn(ds, big)
        if t == n // TR - 1:
            av_ref[...] = av
            ak_ref[...] = ak
        else:
            av_ref[:w, :] += av
            ak_ref[:w, :] += ak
        dq_ref[t*TR:(t+1)*TR, :] = (collect(tn(ds, k)) * HD ** -0.5).astype(bf)

def self_bwd(lens, qkv, grad, rows):
    tok, width3 = qkv.shape
    width = width3 // 3
    n = tok // rows
    lanes = NH * HD
    nb = width // lanes
    spec = lambda off: pl.BlockSpec((n, lanes), lambda r, h, *_: (r, off*nb + h))
    return pl.pallas_call(
        functools.partial(self_bwd_kernel, lens.shape[1]),
        grid_spec=pltpu.PrefetchScalarGridSpec(num_scalar_prefetch=1, grid=(rows, nb, 3),
            in_specs=[spec(0), spec(1), spec(2), spec(0)],
            out_specs=pl.BlockSpec((n, lanes), lambda r, h, p, *_: (r, p*nb + h)),
            scratch_shapes=[pltpu.VMEM((n, n), f32), pltpu.VMEM((n, lanes), bf), pltpu.VMEM((n, lanes), f32), pltpu.VMEM((n, lanes), f32)]),
        out_shape=jax.ShapeDtypeStruct((tok, width3), bf),
        compiler_params=pltpu.CompilerParams(vmem_limit_bytes=48<<20),
        cost_estimate=pl.CostEstimate(flops=5*tok*n*width, bytes_accessed=14*tok*width, transcendentals=tok*n*width//HD//2),
    )(lens, qkv, qkv, qkv, grad)

def seg_bounds(lens_ref, row, segs):
    ends = []
    acc = 0
    for i in range(segs):
        acc = acc + lens_ref[row, i]
        ends.append(acc)
    return ends

def first_seg(ends, pos):
    seg = 0
    for e in ends[:-1]:
        seg = seg + (pos >= e).astype(jnp.int32)
    return seg

def load_keys(ids_ref, row, segs, nret, elen, src_ref, dst_ref):
    for j in range(segs * nret):
        ident = ids_ref[row, j]
        dst_ref[j*elen:(j+1)*elen, :] = src_ref[pl.ds(pl.multiple_of(ident*elen, elen), elen), :]

def lane_seg(ends, t):
    pos = lax.broadcasted_iota(jnp.int32, (1, TR), 1) + t * TR
    seg = jnp.zeros((1, TR), jnp.int32)
    for e in ends[:-1]:
        seg = seg + (pos >= e).astype(jnp.int32)
    return jnp.concatenate([seg]*NH, axis=1)

def row_seg(ends, t, lanes):
    pos = lax.broadcasted_iota(jnp.int32, (TR, 1), 0) + t * TR
    seg = jnp.zeros((TR, 1), jnp.int32)
    for e in ends[:-1]:
        seg = seg + (pos >= e).astype(jnp.int32)
    return seg

def cross_fwd_kernel(segs, nret, elen, lens_ref, ids_ref, q_ref, k_ref, v_ref, o_ref, ks_ref, vs_ref):
    row = pl.program_id(1)
    n = q_ref.shape[0]
    width = nret * elen
    load_keys(ids_ref, row, segs, nret, elen, k_ref, ks_ref)
    load_keys(ids_ref, row, segs, nret, elen, v_ref, vs_ref)
    ends = seg_bounds(lens_ref, row, segs)
    def tile(t, carry):
        rows = pl.ds(pl.multiple_of(t * TR, TR), TR)
        big = spread(q_ref[rows, :], HD ** -0.5)
        lo = first_seg(ends, t * TR)
        hi = first_seg(ends, t * TR + TR - 1)
        qseg = row_seg(ends, t, q_ref.shape[1])
        def pair(s, acc):
            keys = pl.ds(pl.multiple_of(s * width, elen), width)
            p = softmax_t(nt(ks_ref[keys, :], big)).astype(bf)
            got = collect(tn(p, vs_ref[keys, :])).astype(f32)
            return jnp.where(qseg == s, got, acc)
        out = lax.fori_loop(lo, hi + 1, pair, jnp.zeros((TR, q_ref.shape[1]), f32))
        o_ref[rows, :] = out.astype(bf)
        return carry
    lax.fori_loop(0, n // TR, tile, 0)

def cross_fwd(lens, ids, cq, kv, rows, nret, elen):
    tok, width = cq.shape
    n = tok // rows
    lanes = NH * HD
    nb = width // lanes
    segs = lens.shape[1]
    pool = kv.shape[0]
    qspec = pl.BlockSpec((n, lanes), lambda h, r, *_: (r, h))
    kspec = lambda off: pl.BlockSpec((pool, lanes), lambda h, r, *_: (0, off*nb + h))
    keys = segs*nret*elen
    return pl.pallas_call(
        functools.partial(cross_fwd_kernel, segs, nret, elen),
        grid_spec=pltpu.PrefetchScalarGridSpec(num_scalar_prefetch=2, grid=(nb, rows),
            in_specs=[qspec, kspec(0), kspec(1)], out_specs=qspec,
            scratch_shapes=[pltpu.VMEM((keys, lanes), bf)]*2),
        out_shape=jax.ShapeDtypeStruct((tok, width), bf),
        compiler_params=pltpu.CompilerParams(vmem_limit_bytes=48<<20),
        cost_estimate=pl.CostEstimate(flops=2*tok*keys*width, bytes_accessed=8*tok*width, transcendentals=tok*keys*width//HD//2),
    )(lens, ids, cq, kv, kv)

def cross_bwd_kernel(segs, nret, elen, rows_n, lens_ref, ids_ref, q_ref, k_ref, v_ref, g_ref, dq_ref, dkv_ref, ks_ref, vs_ref, ak_ref, av_ref, pk_ref, pv_ref):
    row = pl.program_id(1)

    @pl.when(row < rows_n)
    def _():
        cross_bwd_body(segs, nret, elen, row, lens_ref, ids_ref, q_ref, k_ref, v_ref, g_ref, dq_ref, ks_ref, vs_ref, ak_ref, av_ref, pk_ref, pv_ref)

    @pl.when(row == rows_n - 1)
    def _():
        dkv_ref[...] = pk_ref[...].astype(bf)

    @pl.when(row == rows_n)
    def _():
        dkv_ref[...] = pv_ref[...].astype(bf)

def cross_bwd_body(segs, nret, elen, row, lens_ref, ids_ref, q_ref, k_ref, v_ref, g_ref, dq_ref, ks_ref, vs_ref, ak_ref, av_ref, pk_ref, pv_ref):
    n = q_ref.shape[0]
    width = nret * elen
    load_keys(ids_ref, row, segs, nret, elen, k_ref, ks_ref)
    load_keys(ids_ref, row, segs, nret, elen, v_ref, vs_ref)
    ak_ref[...] = jnp.zeros_like(ak_ref)
    av_ref[...] = jnp.zeros_like(av_ref)
    @pl.when(row == 0)
    def _():
        pk_ref[...] = jnp.zeros_like(pk_ref)
        pv_ref[...] = jnp.zeros_like(pv_ref)
    ends = seg_bounds(lens_ref, row, segs)
    def tile(t, carry):
        rows = pl.ds(pl.multiple_of(t * TR, TR), TR)
        big = spread(q_ref[rows, :], HD ** -0.5)
        gbig = spread(g_ref[rows, :], 1.0)
        lo = first_seg(ends, t * TR)
        hi = first_seg(ends, t * TR + TR - 1)
        qseg = lane_seg(ends, t)
        def pair(s, acc):
            keys = pl.ds(pl.multiple_of(s * width, elen), width)
            k = ks_ref[keys, :]
            sc = nt(k, big)
            top = jnp.max(sc, axis=0, keepdims=True)
            expo = jnp.exp(sc - top)
            inv = 1.0 / jnp.sum(expo, axis=0, keepdims=True)
            inv = jnp.where(qseg == s, inv, 0.0)
            p = expo * inv
            u = p * nt(vs_ref[keys, :], gbig)
            ds = (u - p * jnp.sum(u, axis=0, keepdims=True)).astype(bf)
            av_ref[keys, :] += nn(p.astype(bf), gbig)
            ak_ref[keys, :] += nn(ds, big)
            return acc + collect(tn(ds, k))
        out = lax.fori_loop(lo, hi + 1, pair, jnp.zeros((TR, q_ref.shape[1]), f32))
        dq_ref[rows, :] = (out * HD ** -0.5).astype(bf)
        return carry
    lax.fori_loop(0, n // TR, tile, 0)
    for j in range(segs * nret):
        spot = pl.ds(pl.multiple_of(ids_ref[row, j] * elen, elen), elen)
        pk_ref[spot, :] += ak_ref[j*elen:(j+1)*elen, :]
        pv_ref[spot, :] += av_ref[j*elen:(j+1)*elen, :]

def cross_bwd(lens, ids, cq, kv, grad, rows, nret, elen):
    tok, width = cq.shape
    n = tok // rows
    lanes = NH * HD
    nb = width // lanes
    segs = lens.shape[1]
    pool = kv.shape[0]
    qspec = pl.BlockSpec((n, lanes), lambda h, r, *_: (jnp.minimum(r, rows - 1), h))
    kspec = lambda off: pl.BlockSpec((pool, lanes), lambda h, r, *_: (0, off*nb + h))
    keys = segs*nret*elen
    return pl.pallas_call(
        functools.partial(cross_bwd_kernel, segs, nret, elen, rows),
        grid_spec=pltpu.PrefetchScalarGridSpec(num_scalar_prefetch=2, grid=(nb, rows + 1),
            in_specs=[qspec, kspec(0), kspec(1), qspec], out_specs=[qspec, pl.BlockSpec((pool, lanes), lambda h, r, *_: (0, jnp.where(r < rows, 0, nb) + h))],
            scratch_shapes=[pltpu.VMEM((keys, lanes), bf)]*2+[pltpu.VMEM((keys, lanes), f32)]*2+[pltpu.VMEM((pool, lanes), f32)]*2),
        out_shape=[jax.ShapeDtypeStruct((tok, width), bf)]+[jax.ShapeDtypeStruct(kv.shape, bf)],
        compiler_params=pltpu.CompilerParams(vmem_limit_bytes=56<<20),
        cost_estimate=pl.CostEstimate(flops=5*tok*keys*width, bytes_accessed=14*tok*width, transcendentals=tok*keys*width//HD//2),
    )(lens, ids, cq, kv, kv, grad)


def norm_forward(resid, gain, shift):
    mean_row = jnp.mean(resid, axis=-1, keepdims=True)
    centred = resid - mean_row
    inv = lax.rsqrt(jnp.mean(centred * centred, axis=-1, keepdims=True) + eps_norm)
    normed = centred * inv
    return (normed * gain + shift, normed, inv)


def norm_backward(grad_out, normed, inv, gain):
    scaled = grad_out * gain
    grad_in = inv * (
        scaled
        - jnp.mean(scaled, axis=-1, keepdims=True)
        - normed * jnp.mean(scaled * normed, axis=-1, keepdims=True)
    )
    return (grad_in, jnp.sum(grad_out * normed, axis=0), jnp.sum(grad_out, axis=0))


def gelu_slope(upper):
    cdf = 0.5 * (1.0 + jax.scipy.special.erf(upper * 2.0 ** (-0.5)))
    dens = jnp.exp(-0.5 * upper * upper) * (2.0 * jnp.pi) ** (-0.5)
    return cdf + upper * dens


def swap(value, mask):
    size = lax.axis_size(AXES)
    return lax.ppermute(value, AXES, [(i, i ^ mask) for i in range(size)])


def place_kernel(moves, where_ref, *refs):
    pieces, out_ref, sems = refs[:-2], refs[-2], refs[-1]
    copies = []
    for index, (src, src_row, rows, slot, col, cols) in enumerate(moves):
        first = pl.multiple_of(where_ref[slot], rows)
        copies.append(
            pltpu.make_async_copy(
                pieces[src].at[pl.ds(src_row, rows), :],
                out_ref.at[pl.ds(first, rows), pl.ds(col, cols)],
                sems.at[index],
            )
        )
    for copy in copies:
        copy.start()
    for copy in copies:
        copy.wait()


def place(pieces, where, moves, shape):
    anywhere = pl.BlockSpec(memory_space=pl.ANY)
    return pl.pallas_call(
        functools.partial(place_kernel, tuple(moves)),
        grid_spec=pltpu.PrefetchScalarGridSpec(
            num_scalar_prefetch=1,
            grid=(),
            in_specs=[anywhere] * len(pieces),
            out_specs=anywhere,
            scratch_shapes=[pltpu.SemaphoreType.DMA((len(moves),))],
        ),
        out_shape=jax.ShapeDtypeStruct(shape, bf),
        compiler_params=pltpu.CompilerParams(vmem_limit_bytes=1 << 20),
        cost_estimate=pl.CostEstimate(
            flops=0, bytes_accessed=4 * shape[0] * shape[1], transcendentals=0
        ),
    )(where, *pieces)


def gather_group(shard, me):
    rows, cols = shard.shape
    size = lax.axis_size(AXES)
    low = size // HI
    half = cols // 2
    got = [shard] + [swap(shard, HI * k) for k in range(1, low)]
    hi = me % HI
    lo = me // HI
    if rows % 16:
        lined = jnp.take(jnp.stack(got), lo ^ jnp.arange(low, dtype=jnp.int32), axis=0)
        got, rows, low, lo = [lined.reshape(-1, cols)], rows * low, 1, 0
    pieces = []
    for part, order in ((slice(0, half), (2, 4)), (slice(half, cols), (4, 2))):
        have = {0: jnp.concatenate([g[:, part] for g in got], axis=0)}
        for mask in order + (1,):
            have.update({j | mask: swap(have[j], mask) for j in list(have)})
        pieces += [have[j] for j in range(HI)]
    where = jnp.stack(
        [(hi ^ j) * (low * rows) + (lo ^ k) * rows for j in range(HI) for k in range(low)]
    )
    moves = [
        (p * HI + j, k * rows, rows, j * low + k, p * half, half)
        for p in range(2)
        for j in range(HI)
        for k in range(low)
    ]
    return place(pieces, where, moves, (HI * low * rows, cols))


def gather_passages(own, me):
    rows, cols = own.shape
    group = lax.axis_size("fsdp")
    have = {0: own}
    mask = group // 2
    while mask:
        have.update({j | mask: swap(have[j], mask) for j in list(have)})
        mask //= 2
    index = me % group
    where = jnp.stack([(index ^ j) * rows for j in range(group)])
    moves = [(j, 0, rows, j, 0, cols) for j in range(group)]
    return place([have[j] for j in range(group)], where, moves, (group * rows, cols))


def reduce_passages(whole, me):
    group = lax.axis_size("fsdp")
    blocks = whole.reshape(group, -1, whole.shape[1])
    index = me % group
    have = {j: lax.dynamic_index_in_dim(blocks, index ^ j, 0, keepdims=False) for j in range(group)}
    mask = 1
    while mask < group:
        have = {
            j: (have[j].astype(f32) + swap(have[j | mask].astype(bf), mask).astype(f32))
            for j in have
            if not j & mask
        }
        mask *= 2
    return have[0].astype(bf)


def grad_theirs_kernel(me_ref, x_ref, dz_ref, out_ref, xt_ref):
    block = x_ref.shape[1] // HI

    @pl.when(pl.program_id(0) == 0)
    def _():
        for at, j in enumerate((1, 3, 5, 7)):
            first = pl.multiple_of((j ^ me_ref[0]) * block, block)
            xt_ref[at * block : (at + 1) * block, :] = x_ref[:, pl.ds(first, block)].T

    out_ref[...] = nn(xt_ref[...], dz_ref[...]).astype(bf)


def grad_mine_kernel(half_tiles, me_ref, x_ref, dz_ref, got_ref, keep_ref, sa_ref, sb_ref, xt_ref):
    step = pl.program_id(0)
    block = x_ref.shape[1] // HI

    @pl.when(step == 0)
    def _():
        for at, j in enumerate((0, 2, 4, 6)):
            first = pl.multiple_of((j ^ me_ref[0]) * block, block)
            xt_ref[at * block : (at + 1) * block, :] = x_ref[:, pl.ds(first, block)].T

    full = (nn(xt_ref[...], dz_ref[...]) + got_ref[...].astype(f32)).astype(bf)
    b0, b2, b4, b6 = [full[i * block : (i + 1) * block] for i in range(4)]
    keep_ref[:block, :] = b0

    @pl.when(step < half_tiles)
    def _():
        keep_ref[block:, :] = b4
        sa_ref[:block, :] = b2
        sa_ref[block:, :] = b6

    @pl.when(step >= half_tiles)
    def _():
        keep_ref[block:, :] = b2
        sb_ref[:block, :] = b4
        sb_ref[block:, :] = b6


def second_kernel(half_tiles, keep_ref, ra_ref, rb_ref, out_ref, sa_ref, sb_ref):
    step = pl.program_id(0)
    block = out_ref.shape[0]

    @pl.when(step < half_tiles)
    def _():
        total = (keep_ref[...].astype(f32) + ra_ref[...].astype(f32)).astype(bf)
        out_ref[...] = total[:block]
        sa_ref[...] = total[block:]

    @pl.when(step >= half_tiles)
    def _():
        total = (keep_ref[...].astype(f32) + rb_ref[...].astype(f32)).astype(bf)
        out_ref[...] = total[:block]
        sb_ref[...] = total[block:]


def reduce_group(lhs, dz, me):
    tokens, width = lhs.shape
    cols = dz.shape[1]
    size = lax.axis_size(AXES)
    low = size // HI
    block = width // HI
    tile = min(512, cols // 2)
    tiles = cols // tile
    half_tiles = tiles // 2
    half = cols // 2
    hi = (me % HI).reshape(1)
    big = pltpu.CompilerParams(vmem_limit_bytes=40 << 20)
    cost = pl.CostEstimate(
        flops=tokens * width * cols, bytes_accessed=4 * tokens * cols, transcendentals=0
    )
    whole = pl.BlockSpec((tokens, width), lambda t, *_: (0, 0))
    dz_spec = pl.BlockSpec((tokens, tile), lambda t, *_: (0, t))
    xt = pltpu.VMEM((width // 2, tokens), bf)
    theirs = pl.pallas_call(
        grad_theirs_kernel,
        grid_spec=pltpu.PrefetchScalarGridSpec(
            num_scalar_prefetch=1,
            grid=(tiles,),
            in_specs=[whole, dz_spec],
            out_specs=pl.BlockSpec((width // 2, tile), lambda t, *_: (0, t)),
            scratch_shapes=[xt],
        ),
        out_shape=jax.ShapeDtypeStruct((width // 2, cols), bf),
        compiler_params=big,
        cost_estimate=cost,
    )(hi, lhs, dz)
    got = swap(theirs, 1)
    a_map = lambda t, *_: (0, jnp.minimum(t, half_tiles - 1))
    b_map = lambda t, *_: (0, jnp.maximum(t - half_tiles, 0))
    keep, send_a, send_b = pl.pallas_call(
        functools.partial(grad_mine_kernel, half_tiles),
        grid_spec=pltpu.PrefetchScalarGridSpec(
            num_scalar_prefetch=1,
            grid=(tiles,),
            in_specs=[whole, dz_spec, pl.BlockSpec((width // 2, tile), lambda t, *_: (0, t))],
            out_specs=[
                pl.BlockSpec((2 * block, tile), lambda t, *_: (0, t)),
                pl.BlockSpec((2 * block, tile), a_map),
                pl.BlockSpec((2 * block, tile), b_map),
            ],
            scratch_shapes=[xt],
        ),
        out_shape=[
            jax.ShapeDtypeStruct((2 * block, cols), bf),
            jax.ShapeDtypeStruct((2 * block, half), bf),
            jax.ShapeDtypeStruct((2 * block, half), bf),
        ],
        compiler_params=big,
        cost_estimate=cost,
    )(hi, lhs, dz, got)
    ra = swap(send_a, 2)
    rb = swap(send_b, 4)
    keep, send_a, send_b = pl.pallas_call(
        functools.partial(second_kernel, half_tiles),
        grid=(tiles,),
        in_specs=[
            pl.BlockSpec((2 * block, tile), lambda t: (0, t)),
            pl.BlockSpec((2 * block, tile), a_map),
            pl.BlockSpec((2 * block, tile), b_map),
        ],
        out_specs=[
            pl.BlockSpec((block, tile), lambda t: (0, t)),
            pl.BlockSpec((block, tile), a_map),
            pl.BlockSpec((block, tile), b_map),
        ],
        out_shape=[
            jax.ShapeDtypeStruct((block, cols), bf),
            jax.ShapeDtypeStruct((block, half), bf),
            jax.ShapeDtypeStruct((block, half), bf),
        ],
        compiler_params=pltpu.CompilerParams(vmem_limit_bytes=16 << 20),
        cost_estimate=pl.CostEstimate(
            flops=block * cols, bytes_accessed=12 * block * cols, transcendentals=0
        ),
    )(keep, ra, rb)
    ra = swap(send_a, 4)
    rb = swap(send_b, 2)
    last = keep.astype(f32) + jnp.concatenate([ra, rb], axis=1).astype(f32)
    chunks = last.reshape(low, block // low, cols)
    lo = me // HI
    total = lax.dynamic_index_in_dim(chunks, lo, 0, keepdims=False)
    for k in range(1, low):
        send = lax.dynamic_index_in_dim(chunks, lo ^ k, 0, keepdims=False).astype(bf)
        total = total + swap(send, HI * k).astype(f32)
    return total


def update_kernel(which_ref, basis_ref, g_ref, m_ref, v_ref, w_ref, first_ref, second_ref, new_ref):
    corr_one = 1.0 - beta_one**STEP
    corr_two = 1.0 - beta_two**STEP
    basis = basis_ref[0].astype(bf)
    turned = tn(g_ref[0], basis).T
    first = beta_one * m_ref[...] + (1.0 - beta_one) * turned
    second = beta_two * v_ref[...] + (1.0 - beta_two) * turned * turned
    first_ref[...] = first
    second_ref[...] = second
    step = (first / corr_one) / (jnp.sqrt(second / corr_two) + adam_eps)
    back = nn(basis, step.astype(bf))
    weights = w_ref[...]
    new_ref[...] = weights - rate_mat * (back + decay * weights)


def update(which, bases, grads, first, second, weights):
    count, width, cols = grads.shape
    spec = pl.BlockSpec((width, cols), lambda s, *_: (0, s))
    sds = jax.ShapeDtypeStruct(weights.shape, f32)
    return pl.pallas_call(
        update_kernel,
        grid_spec=pltpu.PrefetchScalarGridSpec(
            num_scalar_prefetch=1,
            grid=(count,),
            in_specs=[
                pl.BlockSpec((1, width, width), lambda s, which_ref: (which_ref[s], 0, 0)),
                pl.BlockSpec((1, width, cols), lambda s, *_: (s, 0, 0)),
                spec,
                spec,
                spec,
            ],
            out_specs=[spec] * 3,
        ),
        out_shape=[sds] * 3,
        compiler_params=pltpu.CompilerParams(vmem_limit_bytes=48 << 20),
        cost_estimate=pl.CostEstimate(
            flops=4 * width * width * cols * count,
            bytes_accessed=4 * count * width * (width + 6 * cols),
            transcendentals=0,
        ),
    )(which, bases, grads, first, second, weights)


def shards(
    hidden_in,
    cotangent,
    seg_lengths,
    retrieved,
    encoder_states,
    master_weights,
    first_moment,
    second_moment,
    slot_block,
    bases,
    vector_params,
    vector_first,
    vector_second,
):
    micro, rows_dev, row_len, width = hidden_in.shape
    segs = seg_lengths.shape[2]
    nret = retrieved.shape[3]
    elen = encoder_states.shape[1]
    size = lax.axis_size(AXES)
    low = size // HI
    me = lax.axis_index(AXES)
    nblk = slot_block.shape[0]
    per_dev = nblk // size
    bcols = master_weights.shape[1] // per_dev
    cols = nblk * bcols
    rp = width // size
    rows = micro * rows_dev
    tokens = rows * row_len
    hidden = (cols - 8 * width) // 2
    nvec = vector_params.shape[0]
    pass_grp = encoder_states.shape[0] * lax.axis_size("fsdp")
    lens = seg_lengths.reshape(rows, segs)
    ids = retrieved.reshape(rows, segs * nret) - lax.axis_index("dp") * pass_grp
    inverse = jnp.zeros((nblk,), jnp.int32).at[slot_block].set(jnp.arange(nblk, dtype=jnp.int32))

    send = (
        master_weights.astype(bf)
        .reshape(HI, low, rp, per_dev, bcols)
        .transpose(1, 0, 3, 2, 4)
        .reshape(size, per_dev, rp, bcols)
    )
    slots = lax.all_to_all(send, AXES, 0, 0, tiled=True).reshape(nblk, rp, bcols)
    natural = jnp.take(slots, inverse, axis=0).transpose(1, 0, 2).reshape(rp, cols)

    part = lax.axis_size(AXES)
    vcols = vector_params.shape[1]
    vecs = lax.dynamic_update_slice(
        jnp.zeros((nvec, vcols * part), bf), vector_params.astype(bf), (0, me * vcols)
    )
    mask = 1
    while mask < size:
        vecs = vecs + swap(vecs, mask)
        mask *= 2
    vecs = vecs.astype(f32)

    enc = gather_passages(encoder_states.reshape(-1, width), me)
    cuts = [0, 3 * width, 5 * width, 8 * width, 8 * width + hidden, cols]
    g_qkv, g_ocq, g_ckvo, w_up, w_dt = [
        gather_group(natural[:, a:b], me) for a, b in zip(cuts[:-1], cuts[1:])
    ]
    w_o, c_q = g_ocq[:, :width], g_ocq[:, width:]
    c_kv, c_o = g_ckvo[:, : 2 * width], g_ckvo[:, 2 * width :]
    zero = jnp.zeros((width,), f32)
    b_up = vecs[13:].reshape(-1)

    x = hidden_in.reshape(tokens, width)
    cot = cotangent.reshape(tokens, width)
    qkv = (nn(x, g_qkv) + jnp.concatenate([vecs[0], zero, vecs[1]])).astype(bf)
    attn = self_fwd(lens, qkv, rows)
    hid_one, normed_one, inv_one = norm_forward(
        x.astype(f32) + nn(attn, w_o) + vecs[2], vecs[3], vecs[4]
    )
    hid_low = hid_one.astype(bf)
    cq = (nn(hid_low, c_q) + vecs[5]).astype(bf)
    kv = (nn(enc, c_kv) + jnp.concatenate([zero, vecs[6]])).astype(bf)
    attn_c = cross_fwd(lens, ids, cq, kv, rows, nret, elen)
    hid_two, normed_two, inv_two = norm_forward(
        hid_one + nn(attn_c, c_o) + vecs[7], vecs[8], vecs[9]
    )
    hid_two_low = hid_two.astype(bf)
    upper = nn(hid_two_low, w_up) + b_up
    act = jax.nn.gelu(upper, approximate=False).astype(bf)
    out, normed_three, inv_three = norm_forward(
        hid_two + nt(act, w_dt) + vecs[10], vecs[11], vecs[12]
    )
    d_resid3, d_g3, d_e3 = norm_backward(cot.astype(f32), normed_three, inv_three, vecs[11])
    d_branch3 = d_resid3.astype(bf)
    d_bdown = jnp.sum(d_branch3.astype(f32), axis=0)
    s_dt = reduce_group(d_branch3, act, me)
    d_upper = (nn(d_branch3, w_dt) * gelu_slope(upper)).astype(bf)
    d_bup = jnp.sum(d_upper.astype(f32), axis=0)
    s_up = reduce_group(hid_two_low, d_upper, me)
    d_hid_two = d_resid3 + nt(d_upper, w_up)
    d_resid2, d_g2, d_e2 = norm_backward(d_hid_two, normed_two, inv_two, vecs[8])
    d_branch2 = d_resid2.astype(bf)
    d_cbo = jnp.sum(d_branch2.astype(f32), axis=0)
    s_co = reduce_group(attn_c, d_branch2, me)
    d_attn_c = nt(d_branch2, c_o).astype(bf)
    g_cq, g_ckv = cross_bwd(lens, ids, cq, kv, d_attn_c, rows, nret, elen)
    d_cbq = jnp.sum(g_cq.astype(f32), axis=0)
    d_cbv = jnp.sum(g_ckv[:, width:].astype(f32), axis=0)
    s_cq = reduce_group(hid_low, g_cq, me)
    s_ckv = reduce_group(enc, g_ckv, me)
    d_hid_one = d_resid2 + nt(g_cq, c_q)
    d_resid1, d_g1, d_e1 = norm_backward(d_hid_one, normed_one, inv_one, vecs[3])
    d_branch1 = d_resid1.astype(bf)
    d_bo = jnp.sum(d_branch1.astype(f32), axis=0)
    s_o = reduce_group(attn, d_branch1, me)
    d_attn = nt(d_branch1, w_o).astype(bf)
    encoder_grad = reduce_passages(nt(g_ckv, c_kv), me)
    g_in = self_bwd(lens, qkv, d_attn, rows)
    d_bq = jnp.sum(g_in[:, :width].astype(f32), axis=0)
    d_bv = jnp.sum(g_in[:, 2 * width :].astype(f32), axis=0)
    s_qkv = reduce_group(x, g_in, me)
    d_x = d_resid1 + nt(g_in, g_qkv)

    vec_grad = jnp.concatenate(
        [
            jnp.stack(
                [d_bq, d_bv, d_bo, d_g1, d_e1, d_cbq, d_cbv, d_cbo, d_g2, d_e2, d_bdown, d_g3, d_e3]
            ),
            d_bup.reshape(-1, width),
        ],
        axis=0,
    )
    mask = 1
    while mask < size:
        vec_grad = vec_grad + swap(vec_grad, mask)
        mask *= 2
    share_vec = lax.dynamic_slice(vec_grad, (0, me * vcols), (nvec, vcols))

    mine = jnp.concatenate([s_qkv, s_o, s_cq, s_ckv, s_co, s_up, s_dt], axis=1).astype(bf)
    blocks = jnp.take(mine.reshape(rp, nblk, bcols).transpose(1, 0, 2), slot_block, axis=0)
    got = lax.all_to_all(blocks.reshape(size, per_dev, rp, bcols), AXES, 0, 0, tiled=True)
    grads = (
        got.reshape(low, HI, per_dev, rp, bcols)
        .transpose(2, 1, 0, 3, 4)
        .reshape(per_dev, width, bcols)
    )
    my_blocks = lax.dynamic_slice(slot_block, (me * per_dev,), (per_dev,))
    bounds = jnp.array([width * j for j in range(1, 9)] + [8 * width + hidden], jnp.int32)
    which = jnp.sum((my_blocks[:, None] * bcols >= bounds[None, :]).astype(jnp.int32), axis=1)
    first_new, second_new, master_new = update(
        which, bases, grads, first_moment, second_moment, master_weights
    )
    corr_one = 1.0 - beta_one**STEP
    corr_two = 1.0 - beta_two**STEP
    vf_new = beta_one * vector_first + (1.0 - beta_one) * share_vec
    vs_new = beta_two * vector_second + (1.0 - beta_two) * share_vec * share_vec
    vec_new = vector_params - rate_vec * (vf_new / corr_one) / (
        jnp.sqrt(vs_new / corr_two) + adam_eps
    )
    return (
        out.astype(bf).reshape(hidden_in.shape),
        d_x.astype(bf).reshape(hidden_in.shape),
        encoder_grad.reshape(encoder_states.shape),
        first_new,
        second_new,
        master_new,
        vf_new,
        vs_new,
        vec_new,
        share_vec,
    )


def solution(mesh):
    spread_rows = P(None, ("dp", "fsdp"), None, None)
    spread_cols = P(None, ("dp", "fsdp"))
    in_specs = (
        spread_rows,
        spread_rows,
        P(None, ("dp", "fsdp"), None),
        spread_rows,
        P(("dp", "fsdp"), None, None),
        spread_cols,
        spread_cols,
        spread_cols,
        P(),
        P(),
        spread_cols,
        spread_cols,
        spread_cols,
    )
    out_specs = (spread_rows, spread_rows, P(("dp", "fsdp"), None, None)) + (spread_cols,) * 7
    return jax.shard_map(shards, mesh=mesh, in_specs=in_specs, out_specs=out_specs, check_vma=False)
```

```python
import functools

import jax
import jax.numpy as jnp
from jax import lax
from jax.experimental import pallas as pl
from jax.experimental.pallas import tpu as pltpu
from jax.sharding import PartitionSpec as P

HD = 64
STEP = 5
NH = 4
TR = 128
TQ = 128
TC = 64
AXES = ("dp", "fsdp")
HI = 8

bf = jnp.bfloat16
f32 = jnp.float32
eps_norm = 1e-05
beta_one = 0.9
beta_two = 0.999
adam_eps = 1e-08
rate_mat = 0.03
rate_vec = 0.25
decay = 0.01

def nt(a,b): return lax.dot_general(a,b,(((1,),(1,)),((),())),preferred_element_type=f32)
def nn(a,b): return lax.dot_general(a,b,(((1,),(0,)),((),())),preferred_element_type=f32)
def tn(a,b): return lax.dot_general(a,b,(((0,),(0,)),((),())),preferred_element_type=f32)

def spread(tile, scale):
    lane_head = lax.broadcasted_iota(jnp.int32, tile.shape, 1) // HD
    tile = tile * jnp.asarray(scale, tile.dtype) if scale != 1.0 else tile
    zero = jnp.zeros_like(tile)
    return jnp.concatenate([jnp.where(lane_head == h, tile, zero) for h in range(NH)], axis=0)

def collect(big):
    tr = big.shape[0] // NH
    lane_head = lax.broadcasted_iota(jnp.int32, (tr, big.shape[1]), 1) // HD
    out = big[:tr]
    for h in range(1, NH):
        out = jnp.where(lane_head == h, big[h*tr:(h+1)*tr], out)
    return out

def softmax_t(scores):
    top = jnp.max(scores, axis=0, keepdims=True)
    expo = jnp.exp(scores - top)
    total = jnp.sum(expo, axis=0, keepdims=True)
    return expo * (1.0 / total)

def seg_of(pos, lens_ref, row, segs):
    end = lens_ref[row, 0]
    seg = (pos >= end).astype(jnp.int32)
    for i in range(1, segs - 1):
        end = end + lens_ref[row, i]
        seg = seg + (pos >= end).astype(jnp.int32)
    return seg

def build_bias(bias_ref, lens_ref, row, segs, flip=False):
    n = bias_ref.shape[0]
    key = lax.broadcasted_iota(jnp.int32, (n, n), 0 if flip else 1)
    que = lax.broadcasted_iota(jnp.int32, (n, n), 1 if flip else 0)
    aseg = seg_of(lax.broadcasted_iota(jnp.int32, (n, 1), 0), lens_ref, row, segs)
    bseg = seg_of(lax.broadcasted_iota(jnp.int32, (1, n), 1), lens_ref, row, segs)
    ok = (aseg == bseg) & (key <= que)
    bias_ref[...] = jnp.where(ok, 0.0, -1e30)

def bias_tile(bias_ref, first, width, tr):
    piece = bias_ref[:width, first:first+tr]
    return jnp.concatenate([piece]*NH, axis=1)

SUBF = 4
def self_fwd_kernel(segs, lens_ref, q_ref, k_ref, v_ref, o_ref, bias_ref):
    row = pl.program_id(0)
    n = q_ref.shape[0]
    lanes = NH * HD
    @pl.when(pl.program_id(1) == 0)
    def _():
        build_bias(bias_ref, lens_ref, row, segs)
    for t in range(n // TQ):
        w = (t + 1) * TQ
        bias = jnp.concatenate([bias_ref[t*TQ:(t+1)*TQ, :w]] * NH, axis=0)
        for b in range(q_ref.shape[1] // lanes):
            cols = slice(b*lanes, (b+1)*lanes)
            big = spread(q_ref[t*TQ:(t+1)*TQ, cols], HD ** -0.5)
            s = nt(big, k_ref[:w, cols]) + bias
            e = jnp.exp(s - jnp.max(s, axis=1, keepdims=True))
            inv = 1.0 / jnp.sum(e, axis=1, keepdims=True)
            o_ref[t*TQ:(t+1)*TQ, cols] = collect(nn(e.astype(bf), v_ref[:w, cols]) * inv).astype(bf)

def self_fwd(lens, qkv, rows):
    tok, width3 = qkv.shape
    width = width3 // 3
    n = tok // rows
    lanes = NH * HD * SUBF
    nb = width // lanes
    spec = lambda off: pl.BlockSpec((n, lanes), lambda r, h, *_: (r, off*nb + h))
    return pl.pallas_call(
        functools.partial(self_fwd_kernel, lens.shape[1]),
        grid_spec=pltpu.PrefetchScalarGridSpec(num_scalar_prefetch=1, grid=(rows, nb),
            in_specs=[spec(0), spec(1), spec(2)], out_specs=spec(0),
            scratch_shapes=[pltpu.VMEM((n, n), f32)]),
        out_shape=jax.ShapeDtypeStruct((tok, width), bf),
        compiler_params=pltpu.CompilerParams(vmem_limit_bytes=48<<20),
        cost_estimate=pl.CostEstimate(flops=2*tok*n*width, bytes_accessed=8*tok*width, transcendentals=tok*n*width//HD//2),
    )(lens, qkv, qkv, qkv)

SUBSB = 4
SUBCB = 4
def self_bwd_kernel(segs, lens_ref, q_ref, k_ref, v_ref, g_ref, out_ref, bias_ref, ak_ref, av_ref):
    row = pl.program_id(0)
    part = pl.program_id(2)

    @pl.when((pl.program_id(1) == 0) & (part == 0))
    def _():
        build_bias(bias_ref, lens_ref, row, segs, True)

    @pl.when(part == 0)
    def _():
        self_bwd_body(q_ref, k_ref, v_ref, g_ref, bias_ref, out_ref, ak_ref, av_ref)

    @pl.when(part == 1)
    def _():
        out_ref[...] = ak_ref[...].astype(bf)

    @pl.when(part == 2)
    def _():
        out_ref[...] = av_ref[...].astype(bf)

def self_bwd_body(q_ref, k_ref, v_ref, g_ref, bias_ref, dq_ref, ak_ref, av_ref):
    n = q_ref.shape[0]
    lanes = NH * HD
    for t in reversed(range(n // TR)):
        w = (t + 1) * TR
        rows = slice(t*TR, (t+1)*TR)
        bias = bias_tile(bias_ref, t*TR, w, TR)
        for b in range(q_ref.shape[1] // lanes):
            cols = slice(b*lanes, (b+1)*lanes)
            big = spread(q_ref[rows, cols], HD ** -0.5)
            gbig = spread(g_ref[rows, cols], 1.0)
            k = k_ref[:w, cols]
            p = softmax_t(nt(k, big) + bias)
            u = p * nt(v_ref[:w, cols], gbig)
            ds = (u - p * jnp.sum(u, axis=0, keepdims=True)).astype(bf)
            av = nn(p.astype(bf), gbig)
            ak = nn(ds, big)
            if t == n // TR - 1:
                av_ref[:, cols] = av
                ak_ref[:, cols] = ak
            else:
                av_ref[:w, cols] += av
                ak_ref[:w, cols] += ak
            dq_ref[rows, cols] = (collect(tn(ds, k)) * HD ** -0.5).astype(bf)

def self_bwd(lens, qkv, grad, rows):
    tok, width3 = qkv.shape
    width = width3 // 3
    n = tok // rows
    lanes = NH * HD * SUBSB
    nb = width // lanes
    spec = lambda off: pl.BlockSpec((n, lanes), lambda r, h, *_: (r, off*nb + h))
    return pl.pallas_call(
        functools.partial(self_bwd_kernel, lens.shape[1]),
        grid_spec=pltpu.PrefetchScalarGridSpec(num_scalar_prefetch=1, grid=(rows, nb, 3),
            in_specs=[spec(0), spec(1), spec(2), spec(0)],
            out_specs=pl.BlockSpec((n, lanes), lambda r, h, p, *_: (r, p*nb + h)),
            scratch_shapes=[pltpu.VMEM((n, n), f32), pltpu.VMEM((n, lanes), f32), pltpu.VMEM((n, lanes), f32)]),
        out_shape=jax.ShapeDtypeStruct((tok, width3), bf),
        compiler_params=pltpu.CompilerParams(vmem_limit_bytes=48<<20),
        cost_estimate=pl.CostEstimate(flops=5*tok*n*width, bytes_accessed=14*tok*width, transcendentals=tok*n*width//HD//2),
    )(lens, qkv, qkv, qkv, grad)

def seg_bounds(lens_ref, row, segs):
    ends = []
    acc = 0
    for i in range(segs):
        acc = acc + lens_ref[row, i]
        ends.append(acc)
    return ends

def first_seg(ends, pos):
    seg = 0
    for e in ends[:-1]:
        seg = seg + (pos >= e).astype(jnp.int32)
    return seg

def load_keys(ids_ref, row, segs, nret, elen, src_ref, dst_ref):
    for j in range(segs * nret):
        ident = ids_ref[row, j]
        dst_ref[j*elen:(j+1)*elen, :] = src_ref[pl.ds(pl.multiple_of(ident*elen, elen), elen), :]

def lane_seg(ends, t):
    pos = lax.broadcasted_iota(jnp.int32, (1, TR), 1) + t * TR
    seg = jnp.zeros((1, TR), jnp.int32)
    for e in ends[:-1]:
        seg = seg + (pos >= e).astype(jnp.int32)
    return jnp.concatenate([seg]*NH, axis=1)

def row_seg(ends, t, lanes):
    pos = lax.broadcasted_iota(jnp.int32, (lanes, 1), 0) + t * lanes
    seg = jnp.zeros((lanes, 1), jnp.int32)
    for e in ends[:-1]:
        seg = seg + (pos >= e).astype(jnp.int32)
    return seg

SUBC = 4
def cross_fwd_kernel(segs, nret, elen, lens_ref, ids_ref, q_ref, k_ref, v_ref, o_ref, ks_ref, vs_ref):
    row = pl.program_id(1)
    n = q_ref.shape[0]
    width = nret * elen
    lanes = NH * HD
    load_keys(ids_ref, row, segs, nret, elen, k_ref, ks_ref)
    load_keys(ids_ref, row, segs, nret, elen, v_ref, vs_ref)
    ends = seg_bounds(lens_ref, row, segs)
    def tile(t, carry):
        rows = pl.ds(pl.multiple_of(t * TC, TC), TC)
        lo = first_seg(ends, t * TC)
        hi = first_seg(ends, t * TC + TC - 1)
        qseg = row_seg(ends, t, TC)
        def pair(s, acc):
            keys = pl.ds(pl.multiple_of(s * width, elen), width)
            got = []
            for b in range(q_ref.shape[1] // lanes):
                cols = slice(b*lanes, (b+1)*lanes)
                big = spread(q_ref[rows, cols], HD ** -0.5)
                sc = nt(big, ks_ref[keys, cols])
                e = jnp.exp(sc - jnp.max(sc, axis=1, keepdims=True))
                inv = 1.0 / jnp.sum(e, axis=1, keepdims=True)
                got.append(collect(nn(e.astype(bf), vs_ref[keys, cols]) * inv))
            for b, g in enumerate(got):
                cols = slice(b*lanes, (b+1)*lanes)
                o_ref[rows, cols] = jnp.where(qseg == s, g, o_ref[rows, cols].astype(f32)).astype(bf)
            return acc
        lax.fori_loop(lo, hi + 1, pair, 0)
        return carry
    lax.fori_loop(0, n // TC, tile, 0)

def cross_fwd(lens, ids, cq, kv, rows, nret, elen):
    tok, width = cq.shape
    n = tok // rows
    lanes = NH * HD * SUBC
    nb = width // lanes
    segs = lens.shape[1]
    pool = kv.shape[0]
    qspec = pl.BlockSpec((n, lanes), lambda h, r, *_: (r, h))
    kspec = lambda off: pl.BlockSpec((pool, lanes), lambda h, r, *_: (0, off*nb + h))
    keys = segs*nret*elen
    return pl.pallas_call(
        functools.partial(cross_fwd_kernel, segs, nret, elen),
        grid_spec=pltpu.PrefetchScalarGridSpec(num_scalar_prefetch=2, grid=(nb, rows),
            in_specs=[qspec, kspec(0), kspec(1)], out_specs=qspec,
            scratch_shapes=[pltpu.VMEM((keys, lanes), bf)]*2),
        out_shape=jax.ShapeDtypeStruct((tok, width), bf),
        compiler_params=pltpu.CompilerParams(vmem_limit_bytes=48<<20),
        cost_estimate=pl.CostEstimate(flops=2*tok*keys*width, bytes_accessed=8*tok*width, transcendentals=tok*keys*width//HD//2),
    )(lens, ids, cq, kv, kv)

def cross_bwd_kernel(segs, nret, elen, rows_n, lens_ref, ids_ref, q_ref, k_ref, v_ref, g_ref, dq_ref, dkv_ref, ks_ref, vs_ref, pk_ref, pv_ref):
    row = pl.program_id(1)

    @pl.when(row == 0)
    def _():
        pk_ref[...] = jnp.zeros_like(pk_ref)
        pv_ref[...] = jnp.zeros_like(pv_ref)

    @pl.when(row < rows_n)
    def _():
        cross_bwd_body(segs, nret, elen, row, lens_ref, ids_ref, q_ref, k_ref, v_ref, g_ref, dq_ref, ks_ref, vs_ref, pk_ref, pv_ref)

    @pl.when(row == rows_n - 1)
    def _():
        dkv_ref[...] = pk_ref[...].astype(bf)

    @pl.when(row == rows_n)
    def _():
        dkv_ref[...] = pv_ref[...].astype(bf)

def cross_bwd_body(segs, nret, elen, row, lens_ref, ids_ref, q_ref, k_ref, v_ref, g_ref, dq_ref, ks_ref, vs_ref, pk_ref, pv_ref):
    n = q_ref.shape[0]
    width = nret * elen
    lanes = NH * HD
    load_keys(ids_ref, row, segs, nret, elen, k_ref, ks_ref)
    load_keys(ids_ref, row, segs, nret, elen, v_ref, vs_ref)
    dq_ref[...] = jnp.zeros_like(dq_ref)
    ends = seg_bounds(lens_ref, row, segs)
    def tile(t, carry):
        rows = pl.ds(pl.multiple_of(t * TR, TR), TR)
        lo = first_seg(ends, t * TR)
        hi = first_seg(ends, t * TR + TR - 1)
        qseg = lane_seg(ends, t)
        kseg = row_seg(ends, t, TR)
        def pair(s, acc):
            keys = pl.ds(pl.multiple_of(s * width, elen), width)
            spots = [pl.ds(pl.multiple_of(ids_ref[row, s * nret + j] * elen, elen), elen) for j in range(nret)]
            made = []
            for b in range(q_ref.shape[1] // lanes):
                cols = slice(b*lanes, (b+1)*lanes)
                big = spread(q_ref[rows, cols], HD ** -0.5)
                gbig = spread(g_ref[rows, cols], 1.0)
                k = ks_ref[keys, cols]
                sc = nt(k, big)
                expo = jnp.exp(sc - jnp.max(sc, axis=0, keepdims=True))
                inv = 1.0 / jnp.sum(expo, axis=0, keepdims=True)
                p = expo * jnp.where(qseg == s, inv, 0.0)
                u = p * nt(vs_ref[keys, cols], gbig)
                ds = (u - p * jnp.sum(u, axis=0, keepdims=True)).astype(bf)
                made.append((cols, nn(p.astype(bf), gbig), nn(ds, big), collect(tn(ds, k)) * HD ** -0.5))
            for cols, av, ak, dq in made:
                for j, spot in enumerate(spots):
                    pv_ref[spot, cols] += av[j*elen:(j+1)*elen]
                    pk_ref[spot, cols] += ak[j*elen:(j+1)*elen]
                dq_ref[rows, cols] = jnp.where(kseg == s, dq, dq_ref[rows, cols].astype(f32)).astype(bf)
            return acc
        lax.fori_loop(lo, hi + 1, pair, 0)
        return carry
    lax.fori_loop(0, n // TR, tile, 0)

def cross_bwd(lens, ids, cq, kv, grad, rows, nret, elen):
    tok, width = cq.shape
    n = tok // rows
    pool = kv.shape[0]
    lanes = NH * HD * (SUBCB if pool <= 2048 else SUBCB // 2)
    nb = width // lanes
    segs = lens.shape[1]
    qspec = pl.BlockSpec((n, lanes), lambda h, r, *_: (jnp.minimum(r, rows - 1), h))
    kspec = lambda off: pl.BlockSpec((pool, lanes), lambda h, r, *_: (0, off*nb + h))
    keys = segs*nret*elen
    return pl.pallas_call(
        functools.partial(cross_bwd_kernel, segs, nret, elen, rows),
        grid_spec=pltpu.PrefetchScalarGridSpec(num_scalar_prefetch=2, grid=(nb, rows + 1),
            in_specs=[qspec, kspec(0), kspec(1), qspec],
            out_specs=[qspec, pl.BlockSpec((pool, lanes), lambda h, r, *_: (0, jnp.where(r < rows, 0, nb) + h))],
            scratch_shapes=[pltpu.VMEM((keys, lanes), bf)]*2+[pltpu.VMEM((pool, lanes), f32)]*2),
        out_shape=[jax.ShapeDtypeStruct((tok, width), bf), jax.ShapeDtypeStruct(kv.shape, bf)],
        compiler_params=pltpu.CompilerParams(vmem_limit_bytes=60<<20),
        cost_estimate=pl.CostEstimate(flops=5*tok*keys*width, bytes_accessed=14*tok*width, transcendentals=tok*keys*width//HD//2),
    )(lens, ids, cq, kv, kv, grad)


def norm_forward(resid, gain, shift):
    mean_row = jnp.mean(resid, axis=-1, keepdims=True)
    centred = resid - mean_row
    inv = lax.rsqrt(jnp.mean(centred * centred, axis=-1, keepdims=True) + eps_norm)
    normed = centred * inv
    return (normed * gain + shift, normed, inv)


def norm_backward(grad_out, normed, inv, gain):
    scaled = grad_out * gain
    grad_in = inv * (
        scaled
        - jnp.mean(scaled, axis=-1, keepdims=True)
        - normed * jnp.mean(scaled * normed, axis=-1, keepdims=True)
    )
    return (grad_in, jnp.sum(grad_out * normed, axis=0), jnp.sum(grad_out, axis=0))


def swap(value, mask):
    size = lax.axis_size(AXES)
    return lax.ppermute(value, AXES, [(i, i ^ mask) for i in range(size)])


def place_kernel(moves, count, where_ref, *refs):
    pieces, outs, sems = refs[: -count - 1], refs[-count - 1 : -1], refs[-1]
    copies = []
    for index, (src, row, rows, col, cols, slot, out, to) in enumerate(moves):
        first = pl.multiple_of(where_ref[slot], rows)
        copies.append(
            pltpu.make_async_copy(
                pieces[src].at[pl.ds(row, rows), pl.ds(col, cols)],
                outs[out].at[pl.ds(first, rows), pl.ds(to, cols)],
                sems.at[index],
            )
        )
    for copy in copies:
        copy.start()
    for copy in copies:
        copy.wait()


def place(pieces, where, moves, shapes):
    anywhere = pl.BlockSpec(memory_space=pl.ANY)
    total = sum(a * b for a, b in shapes)
    return pl.pallas_call(
        functools.partial(place_kernel, tuple(moves), len(shapes)),
        grid_spec=pltpu.PrefetchScalarGridSpec(
            num_scalar_prefetch=1,
            grid=(),
            in_specs=[anywhere] * len(pieces),
            out_specs=[anywhere] * len(shapes),
            scratch_shapes=[pltpu.SemaphoreType.DMA((len(moves),))],
        ),
        out_shape=[jax.ShapeDtypeStruct(shape, bf) for shape in shapes],
        compiler_params=pltpu.CompilerParams(vmem_limit_bytes=1 << 20),
        cost_estimate=pl.CostEstimate(flops=0, bytes_accessed=4 * total, transcendentals=0),
    )(where, *pieces)


class Gather:
    def __init__(self, shard, widths, me):
        self.rows, self.cols = shard.shape
        self.widths = widths
        self.me = me
        self.low = lax.axis_size(AXES) // HI
        self.shard = shard

    def far(self):
        self.got = [self.shard] + [swap(self.shard, HI * k) for k in range(1, self.low)]

    def first(self):
        half = self.cols // 2
        got, self.sub = self.got, self.low
        if self.rows % 16:
            order = (self.me // HI) ^ jnp.arange(self.low, dtype=jnp.int32)
            got = [jnp.take(jnp.stack(got), order, axis=0).reshape(-1, self.cols)]
            self.sub = 1
        self.own = [jnp.concatenate([g[:, p * half : (p + 1) * half] for g in got]) for p in (0, 1)]
        self.near = [swap(self.own[p], 2 << p) for p in (0, 1)]

    def second(self):
        self.wide = [jnp.concatenate([self.own[p], self.near[p]]) for p in (0, 1)]
        self.across = [swap(self.wide[p], 4 >> p) for p in (0, 1)]
        self.pair = [swap(self.wide[p], 1) for p in (0, 1)]

    def third(self):
        self.pair2 = [swap(self.across[p], 1) for p in (0, 1)]

    def finish(self):
        half = self.cols // 2
        block = self.low * self.rows
        rows = block // self.sub
        hi = self.me % HI
        lo = self.me // HI if self.sub > 1 else 0
        where = jnp.stack(
            [(hi ^ j) * block + (lo ^ k) * rows for j in range(HI) for k in range(self.sub)]
        )
        pieces, moves = [], []
        for p in (0, 1):
            near, across = 2 << p, 4 >> p
            for value, base in (
                (self.wide[p], 0),
                (self.across[p], across),
                (self.pair[p], 1),
                (self.pair2[p], across | 1),
            ):
                for i, j in enumerate((base, base | near)):
                    for k in range(self.sub):
                        start = 0
                        for out, width in enumerate(self.widths):
                            lower = max(start, p * half)
                            upper = min(start + width, (p + 1) * half)
                            if lower < upper:
                                moves.append(
                                    (
                                        len(pieces),
                                        i * block + k * rows,
                                        rows,
                                        lower - p * half,
                                        upper - lower,
                                        j * self.sub + k,
                                        out,
                                        lower - start,
                                    )
                                )
                            start += width
                pieces.append(value)
        return place(pieces, where, moves, [(HI * block, width) for width in self.widths])


class Passages:
    def __init__(self, own, me):
        self.have = {0: own}
        self.me = me

    def across(self):
        mask = lax.axis_size("fsdp") // 2
        while mask > 1:
            self.have.update({j | mask: swap(self.have[j], mask) for j in list(self.have)})
            mask //= 2

    def pair(self):
        self.have.update({j | 1: swap(self.have[j], 1) for j in list(self.have)})

    def finish(self):
        group = lax.axis_size("fsdp")
        rows, cols = self.have[0].shape
        index = self.me % group
        where = jnp.stack([(index ^ j) * rows for j in range(group)])
        moves = [(j, 0, rows, 0, cols, j, 0, 0) for j in range(group)]
        return place([self.have[j] for j in range(group)], where, moves, [(group * rows, cols)])[0]


class ReducePassages:
    def __init__(self, whole, me):
        self.group = lax.axis_size("fsdp")
        blocks = whole.reshape(self.group, -1, whole.shape[1])
        index = me % self.group
        self.have = {
            j: lax.dynamic_index_in_dim(blocks, index ^ j, 0, keepdims=False)
            for j in range(self.group)
        }
        self.mask = 1
        self.send()

    def send(self):
        self.got = {
            j: swap(self.have[j | self.mask], self.mask) for j in self.have if not j & self.mask
        }

    def step(self):
        self.have = {
            j: (self.have[j].astype(f32) + got.astype(f32)).astype(bf)
            for j, got in self.got.items()
        }
        self.mask *= 2
        if self.mask < self.group:
            self.send()


def grad_theirs_kernel(me_ref, x_ref, dz_ref, out_ref, xt_ref):
    block = x_ref.shape[1] // HI

    @pl.when(pl.program_id(0) == 0)
    def _():
        for at, j in enumerate((1, 3, 5, 7)):
            first = pl.multiple_of((j ^ me_ref[0]) * block, block)
            xt_ref[at * block : (at + 1) * block, :] = x_ref[:, pl.ds(first, block)].T

    out_ref[...] = nn(xt_ref[...], dz_ref[...]).astype(bf)


def grad_mine_kernel(half_tiles, me_ref, x_ref, dz_ref, got_ref, keep_ref, sa_ref, sb_ref, xt_ref):
    step = pl.program_id(0)
    block = x_ref.shape[1] // HI

    @pl.when(step == 0)
    def _():
        for at, j in enumerate((0, 2, 4, 6)):
            first = pl.multiple_of((j ^ me_ref[0]) * block, block)
            xt_ref[at * block : (at + 1) * block, :] = x_ref[:, pl.ds(first, block)].T

    full = (nn(xt_ref[...], dz_ref[...]) + got_ref[...].astype(f32)).astype(bf)
    b0, b2, b4, b6 = [full[i * block : (i + 1) * block] for i in range(4)]
    keep_ref[:block, :] = b0

    @pl.when(step < half_tiles)
    def _():
        keep_ref[block:, :] = b4
        sa_ref[:block, :] = b2
        sa_ref[block:, :] = b6

    @pl.when(step >= half_tiles)
    def _():
        keep_ref[block:, :] = b2
        sb_ref[:block, :] = b4
        sb_ref[block:, :] = b6


def second_kernel(half_tiles, keep_ref, ra_ref, rb_ref, out_ref, sa_ref, sb_ref):
    step = pl.program_id(0)
    block = out_ref.shape[0]

    @pl.when(step < half_tiles)
    def _():
        total = (keep_ref[...].astype(f32) + ra_ref[...].astype(f32)).astype(bf)
        out_ref[...] = total[:block]
        sa_ref[...] = total[block:]

    @pl.when(step >= half_tiles)
    def _():
        total = (keep_ref[...].astype(f32) + rb_ref[...].astype(f32)).astype(bf)
        out_ref[...] = total[:block]
        sb_ref[...] = total[block:]


def third_kernel(half_tiles, rp, lo_ref, keep_ref, ra_ref, rb_ref, *refs):
    outs, sum_ref = refs[:-1], refs[-1]
    step = pl.program_id(0)

    @pl.when(step < half_tiles)
    def _():
        sum_ref[...] = keep_ref[...].astype(f32) + ra_ref[...].astype(f32)

    @pl.when(step >= half_tiles)
    def _():
        sum_ref[...] = keep_ref[...].astype(f32) + rb_ref[...].astype(f32)

    for k, out in enumerate(outs):
        first = pl.multiple_of((lo_ref[0] ^ k) * rp, rp)
        out[...] = sum_ref[pl.ds(first, rp), :].astype(bf)


class Reduce:
    def __init__(self, lhs, dz, me):
        self.lhs, self.dz = lhs, dz
        self.tokens, self.width = lhs.shape
        self.cols = dz.shape[1]
        self.low = lax.axis_size(AXES) // HI
        self.block = self.width // HI
        self.tile = min(512, self.cols // 2)
        self.tiles = self.cols // self.tile
        self.half_tiles = self.tiles // 2
        self.lo = me // HI
        self.hi = (me % HI).reshape(1)
        self.a_map = lambda t, *_: (0, jnp.minimum(t, self.half_tiles - 1))
        self.b_map = lambda t, *_: (0, jnp.maximum(t - self.half_tiles, 0))
        self.big = pltpu.CompilerParams(vmem_limit_bytes=40 << 20)
        self.cost = pl.CostEstimate(
            flops=self.tokens * self.width * self.cols,
            bytes_accessed=4 * self.tokens * self.cols,
            transcendentals=0,
        )

    def spec(self, rows, index=None):
        return pl.BlockSpec((rows, self.tile), index or (lambda t, *_: (0, t)))

    def shape(self, rows, cols):
        return jax.ShapeDtypeStruct((rows, cols), bf)

    def theirs(self):
        half = self.width // 2
        out = pl.pallas_call(
            grad_theirs_kernel,
            grid_spec=pltpu.PrefetchScalarGridSpec(
                num_scalar_prefetch=1,
                grid=(self.tiles,),
                in_specs=[
                    pl.BlockSpec((self.tokens, self.width), lambda t, *_: (0, 0)),
                    self.spec(self.tokens),
                ],
                out_specs=self.spec(half),
                scratch_shapes=[pltpu.VMEM((half, self.tokens), bf)],
            ),
            out_shape=self.shape(half, self.cols),
            compiler_params=self.big,
            cost_estimate=self.cost,
        )(self.hi, self.lhs, self.dz)
        self.got = swap(out, 1)
        return out

    def mine(self):
        half = self.width // 2
        two = 2 * self.block
        self.keep, send_a, send_b = pl.pallas_call(
            functools.partial(grad_mine_kernel, self.half_tiles),
            grid_spec=pltpu.PrefetchScalarGridSpec(
                num_scalar_prefetch=1,
                grid=(self.tiles,),
                in_specs=[
                    pl.BlockSpec((self.tokens, self.width), lambda t, *_: (0, 0)),
                    self.spec(self.tokens),
                    self.spec(half),
                ],
                out_specs=[self.spec(two), self.spec(two, self.a_map), self.spec(two, self.b_map)],
                scratch_shapes=[pltpu.VMEM((half, self.tokens), bf)],
            ),
            out_shape=[
                self.shape(two, self.cols),
                self.shape(two, self.cols // 2),
                self.shape(two, self.cols // 2),
            ],
            compiler_params=self.big,
            cost_estimate=self.cost,
        )(self.hi, self.lhs, self.dz, self.got)
        self.ra, self.rb = swap(send_a, 2), swap(send_b, 4)
        return self.keep

    def second(self):
        two, one = 2 * self.block, self.block
        self.keep, send_a, send_b = pl.pallas_call(
            functools.partial(second_kernel, self.half_tiles),
            grid=(self.tiles,),
            in_specs=[self.spec(two), self.spec(two, self.a_map), self.spec(two, self.b_map)],
            out_specs=[self.spec(one), self.spec(one, self.a_map), self.spec(one, self.b_map)],
            out_shape=[
                self.shape(one, self.cols),
                self.shape(one, self.cols // 2),
                self.shape(one, self.cols // 2),
            ],
            compiler_params=pltpu.CompilerParams(vmem_limit_bytes=16 << 20),
            cost_estimate=pl.CostEstimate(
                flops=one * self.cols, bytes_accessed=12 * one * self.cols, transcendentals=0
            ),
        )(self.keep, self.ra, self.rb)
        self.ra, self.rb = swap(send_a, 4), swap(send_b, 2)
        return self.keep

    def third(self):
        one = self.block
        rp = one // self.low
        if rp % 16:
            last = self.keep.astype(f32) + jnp.concatenate([self.ra, self.rb], axis=1).astype(f32)
            chunks = last.reshape(self.low, rp, self.cols)
            parts = [
                lax.dynamic_index_in_dim(chunks, self.lo ^ k, 0, keepdims=False).astype(bf)
                for k in range(self.low)
            ]
        else:
            parts = pl.pallas_call(
                functools.partial(third_kernel, self.half_tiles, rp),
                grid_spec=pltpu.PrefetchScalarGridSpec(
                    num_scalar_prefetch=1,
                    grid=(self.tiles,),
                    in_specs=[
                        self.spec(one),
                        self.spec(one, self.a_map),
                        self.spec(one, self.b_map),
                    ],
                    out_specs=[self.spec(rp)] * self.low,
                    scratch_shapes=[pltpu.VMEM((one, self.tile), f32)],
                ),
                out_shape=[self.shape(rp, self.cols)] * self.low,
                compiler_params=pltpu.CompilerParams(vmem_limit_bytes=16 << 20),
                cost_estimate=pl.CostEstimate(
                    flops=one * self.cols, bytes_accessed=8 * one * self.cols, transcendentals=0
                ),
            )(self.lo.reshape(1), self.keep, self.ra, self.rb)
        self.parts = [parts[0]] + [swap(parts[k], HI * k) for k in range(1, self.low)]
        return parts[0]

    def last(self):
        return sum(part.astype(f32) for part in self.parts).astype(bf)


def up_kernel(h_ref, w_ref, b_ref, act_ref, slope_ref):
    upper = nn(h_ref[...], w_ref[...]) + b_ref[...]
    dens = jnp.exp(-0.5 * upper * upper)
    t = 1.0 / (1.0 + (0.3275911 * 2.0**-0.5) * jnp.abs(upper))
    poly = 0.5 * 1.061405429
    for coef in (-1.453152027, 1.421413741, -0.284496736, 0.254829592):
        poly = poly * t + 0.5 * coef
    tail = poly * t * dens
    cdf = jnp.where(upper < 0.0, tail, 1.0 - tail)
    act_ref[...] = (upper * cdf).astype(bf)
    slope_ref[...] = (cdf + upper * dens * (2.0 * jnp.pi) ** -0.5).astype(bf)


def up_project(h, w, b):
    tokens, width = h.shape
    cols = w.shape[1]
    tile = 512
    spec = pl.BlockSpec((tokens, tile), lambda t: (0, t))
    return pl.pallas_call(
        up_kernel,
        grid=(cols // tile,),
        in_specs=[
            pl.BlockSpec((tokens, width), lambda t: (0, 0)),
            pl.BlockSpec((width, tile), lambda t: (0, t)),
            pl.BlockSpec((1, tile), lambda t: (0, t)),
        ],
        out_specs=[spec, spec],
        out_shape=[jax.ShapeDtypeStruct((tokens, cols), bf)] * 2,
        compiler_params=pltpu.CompilerParams(vmem_limit_bytes=40 << 20),
        cost_estimate=pl.CostEstimate(
            flops=2 * tokens * width * cols,
            bytes_accessed=4 * tokens * cols + 2 * width * cols,
            transcendentals=tokens * cols,
        ),
    )(h, w, b)


def update_kernel(which_ref, basis_ref, g_ref, m_ref, v_ref, w_ref, first_ref, second_ref, new_ref):
    corr_one = 1.0 - beta_one**STEP
    corr_two = 1.0 - beta_two**STEP
    basis = basis_ref[0].astype(bf)
    turned = tn(g_ref[0], basis).T
    first = beta_one * m_ref[...] + (1.0 - beta_one) * turned
    second = beta_two * v_ref[...] + (1.0 - beta_two) * turned * turned
    first_ref[...] = first
    second_ref[...] = second
    step = (first / corr_one) / (jnp.sqrt(second / corr_two) + adam_eps)
    back = nn(basis, step.astype(bf))
    weights = w_ref[...]
    new_ref[...] = weights - rate_mat * (back + decay * weights)


def update(which, bases, grads, first, second, weights):
    count, width, cols = grads.shape
    spec = pl.BlockSpec((width, cols), lambda s, *_: (0, s))
    sds = jax.ShapeDtypeStruct(weights.shape, f32)
    return pl.pallas_call(
        update_kernel,
        grid_spec=pltpu.PrefetchScalarGridSpec(
            num_scalar_prefetch=1,
            grid=(count,),
            in_specs=[
                pl.BlockSpec((1, width, width), lambda s, which_ref: (which_ref[s], 0, 0)),
                pl.BlockSpec((1, width, cols), lambda s, *_: (s, 0, 0)),
                spec,
                spec,
                spec,
            ],
            out_specs=[spec] * 3,
        ),
        out_shape=[sds] * 3,
        compiler_params=pltpu.CompilerParams(vmem_limit_bytes=48 << 20),
        cost_estimate=pl.CostEstimate(
            flops=4 * width * width * cols * count,
            bytes_accessed=4 * count * width * (width + 6 * cols),
            transcendentals=0,
        ),
    )(which, bases, grads, first, second, weights)


def shards(
    hidden_in,
    cotangent,
    seg_lengths,
    retrieved,
    encoder_states,
    master_weights,
    first_moment,
    second_moment,
    slot_block,
    bases,
    vector_params,
    vector_first,
    vector_second,
):
    micro, rows_dev, row_len, width = hidden_in.shape
    segs = seg_lengths.shape[2]
    nret = retrieved.shape[3]
    elen = encoder_states.shape[1]
    size = lax.axis_size(AXES)
    low = size // HI
    me = lax.axis_index(AXES)
    nblk = slot_block.shape[0]
    per_dev = nblk // size
    bcols = master_weights.shape[1] // per_dev
    cols = nblk * bcols
    rp = width // size
    rows = micro * rows_dev
    tokens = rows * row_len
    hidden = (cols - 8 * width) // 2
    nvec = vector_params.shape[0]
    pass_grp = encoder_states.shape[0] * lax.axis_size("fsdp")
    lens = seg_lengths.reshape(rows, segs)
    ids = retrieved.reshape(rows, segs * nret) - lax.axis_index("dp") * pass_grp
    inverse = jnp.zeros((nblk,), jnp.int32).at[slot_block].set(jnp.arange(nblk, dtype=jnp.int32))

    passages = Passages(encoder_states.reshape(-1, width), me)
    passages.across()
    send = (
        master_weights.astype(bf)
        .reshape(HI, low, rp, per_dev, bcols)
        .transpose(1, 0, 3, 2, 4)
        .reshape(size, per_dev, rp, bcols)
    )
    slots = lax.all_to_all(send, AXES, 0, 0, tiled=True).reshape(nblk, rp, bcols)
    natural = jnp.take(slots, inverse, axis=0).transpose(1, 0, 2).reshape(rp, cols)

    vcols = vector_params.shape[1]
    vec_pad = jnp.pad(vector_params.astype(bf).T, ((0, 0), (0, 2 * bcols - nvec)))
    zero = jnp.zeros((width,), f32)
    x = hidden_in.reshape(tokens, width)
    cot = cotangent.reshape(tokens, width)

    cuts = [0, 3 * width, 7 * width, 8 * width + hidden, cols]
    parts = [natural[:, i:j] for i, j in zip(cuts[:-1], cuts[1:])]
    parts[0] = jnp.concatenate([parts[0], vec_pad], axis=1)
    widths = [(3 * width, 2 * bcols), (width, width, 2 * width), (width, hidden), (hidden,)]
    ga, gb, gc, gd = [Gather(p, w, me) for p, w in zip(parts, widths)]

    def after(value, *done):
        return lax.optimization_barrier((value, done))[0]

    ga.far()
    ga.first()
    gb.shard = after(gb.shard, ga.own)
    gb.far()
    ga.second()
    gb.got = after(gb.got, ga.wide)
    gb.first()
    gc.shard = after(gc.shard, gb.own)
    gc.far()
    ga.across = after(ga.across, gb.own)
    ga.third()
    gb.near = after(gb.near, gc.shard)
    gb.second()
    gc.got = after(gc.got, gb.wide)
    gc.first()
    ga.pair2, gd.shard = after((ga.pair2, gd.shard), gc.own)
    gd.far()
    passages.have = after(passages.have, ga.pair2)
    passages.pair()
    w_qkv, w_vec = ga.finish()
    vecs = (
        w_vec[:, :nvec].reshape(HI, low, rp, nvec).transpose(3, 1, 0, 2).reshape(nvec, width)
    ).astype(f32)

    b_up = vecs[13:].reshape(1, -1)
    qkv = (nn(x, w_qkv) + jnp.concatenate([vecs[0], zero, vecs[1]])).astype(bf)
    passages.have = after(passages.have, qkv)
    enc = passages.finish()
    attn = self_fwd(lens, after(qkv, enc), rows)
    gb.across, gc.near, gd.got = after((gb.across, gc.near, gd.got), attn)
    gb.third()
    gc.second()
    gd.got = after(gd.got, gc.wide)
    gd.first()
    gb.pair2 = after(gb.pair2, gd.own)
    w_o, c_q, c_kv = gb.finish()
    hid_one, normed_one, inv_one = norm_forward(
        x.astype(f32) + nn(attn, w_o) + vecs[2], vecs[3], vecs[4]
    )
    hid_low = hid_one.astype(bf)
    cq = (nn(hid_low, c_q) + vecs[5]).astype(bf)
    kv = (nn(after(enc, cq), c_kv) + jnp.concatenate([zero, vecs[6]])).astype(bf)
    attn_c = cross_fwd(lens, ids, cq, kv, rows, nret, elen)
    gc.across, gd.near = after((gc.across, gd.near), attn_c)
    gc.third()
    gd.second()
    gc.pair2 = after(gc.pair2, gd.wide)
    c_o, w_up = gc.finish()
    hid_two, normed_two, inv_two = norm_forward(
        hid_one + nn(attn_c, c_o) + vecs[7], vecs[8], vecs[9]
    )
    hid_two_low = hid_two.astype(bf)
    act, slope = up_project(hid_two_low, w_up, b_up)
    gd.across = after(gd.across, act)
    gd.third()
    (w_dt,) = gd.finish()
    out, normed_three, inv_three = norm_forward(
        hid_two + nt(act, w_dt) + vecs[10], vecs[11], vecs[12]
    )

    d_resid3, d_g3, d_e3 = norm_backward(cot.astype(f32), normed_three, inv_three, vecs[11])
    d_branch3 = d_resid3.astype(bf)
    d_bdown = jnp.sum(d_branch3.astype(f32), axis=0)
    r_dt = Reduce(d_branch3, act, me)
    done = r_dt.theirs()
    d_branch3 = after(d_branch3, done)
    d_upper = (nn(d_branch3, w_dt) * slope.astype(f32)).astype(bf)
    d_bup = jnp.sum(d_upper.astype(f32), axis=0)
    r_dt.got = after(r_dt.got, d_upper)
    done = r_dt.mine()
    r_up = Reduce(hid_two_low, after(d_upper, done), me)
    done = r_up.theirs()
    d_upper = after(d_upper, done)
    d_hid_two = d_resid3 + nt(d_upper, w_up)
    d_resid2, d_g2, d_e2 = norm_backward(d_hid_two, normed_two, inv_two, vecs[8])
    d_branch2 = d_resid2.astype(bf)
    d_cbo = jnp.sum(d_branch2.astype(f32), axis=0)
    r_dt.ra = after(r_dt.ra, d_branch2)
    done = r_dt.second()
    r_up.got = after(r_up.got, done)
    done = r_up.mine()
    d_branch2 = after(d_branch2, done)
    d_attn_c = nt(d_branch2, c_o).astype(bf)
    r_co = Reduce(attn_c, after(d_branch2, d_attn_c), me)
    done = r_co.theirs()
    r_dt.ra = after(r_dt.ra, done)
    done = r_dt.third()
    r_up.ra = after(r_up.ra, done)
    done = r_up.second()
    g_cq, g_ckv = cross_bwd(lens, ids, cq, kv, after(d_attn_c, done), rows, nret, elen)
    r_dt.parts, r_co.got = after((r_dt.parts, r_co.got), g_cq)
    s_dt = r_dt.last()
    r_co.got = after(r_co.got, s_dt)
    done = r_co.mine()
    r_up.ra = after(r_up.ra, done)
    done = r_up.third()
    r_cq = Reduce(hid_low, after(g_cq, done), me)
    done = r_cq.theirs()
    r_ckv = Reduce(enc, after(g_ckv, done), me)
    done = r_ckv.theirs()
    d_cbq = jnp.sum(g_cq.astype(f32), axis=0)
    d_cbv = jnp.sum(g_ckv[:, width:].astype(f32), axis=0)
    d_hid_one = d_resid2 + nt(after(g_cq, done), c_q)
    d_resid1, d_g1, d_e1 = norm_backward(d_hid_one, normed_one, inv_one, vecs[3])
    d_branch1 = d_resid1.astype(bf)
    d_bo = jnp.sum(d_branch1.astype(f32), axis=0)
    r_up.parts, r_co.ra = after((r_up.parts, r_co.ra), d_branch1)
    s_up = r_up.last()
    r_co.ra = after(r_co.ra, s_up)
    done = r_co.second()
    r_cq.got = after(r_cq.got, done)
    done = r_cq.mine()
    r_ckv.got = after(r_ckv.got, done)
    done = r_ckv.mine()
    r_o = Reduce(attn, after(d_branch1, done), me)
    done = r_o.theirs()
    d_attn = nt(after(d_branch1, done), w_o).astype(bf)
    d_enc = nt(after(g_ckv, d_attn), c_kv).astype(bf)
    r_enc = ReducePassages(d_enc, me)
    r_co.ra = after(r_co.ra, r_enc.have)
    done = r_co.third()
    r_cq.ra = after(r_cq.ra, done)
    done = r_cq.second()
    r_ckv.ra = after(r_ckv.ra, done)
    done = r_ckv.second()
    r_o.got = after(r_o.got, done)
    done = r_o.mine()
    r_enc.got = after(r_enc.got, done)
    r_enc.step()
    r_co.parts = after(r_co.parts, r_enc.have)
    s_co = r_co.last()
    g_in = self_bwd(lens, qkv, after(d_attn, r_enc.have, s_co), rows)
    r_in = Reduce(x, g_in, me)
    done = r_in.theirs()
    r_cq.ra, r_ckv.ra, r_o.ra = after((r_cq.ra, r_ckv.ra, r_o.ra), done)
    done = r_cq.third(), r_ckv.third(), r_o.second()
    g_in = after(g_in, done)
    d_bq = jnp.sum(g_in[:, :width].astype(f32), axis=0)
    d_bv = jnp.sum(g_in[:, 2 * width :].astype(f32), axis=0)
    r_in.got = after(r_in.got, d_bq, d_bv)
    done = r_in.mine()
    while r_enc.mask < r_enc.group:
        r_enc.step()
    encoder_grad = r_enc.have[0]
    r_cq.parts, r_ckv.parts = after((r_cq.parts, r_ckv.parts), done)
    s_cq, s_ckv = r_cq.last(), r_ckv.last()
    done = done, s_cq, s_ckv
    vec_grad = jnp.concatenate(
        [
            jnp.stack(
                [d_bq, d_bv, d_bo, d_g1, d_e1, d_cbq, d_cbv, d_cbo, d_g2, d_e2, d_bdown, d_g3, d_e3]
            ),
            d_bup.reshape(-1, width),
        ],
        axis=0,
    )
    g_in = after(g_in, done)
    d_x = (d_resid1 + nt(g_in, w_qkv)).astype(bf)
    r_o.ra = after(r_o.ra, d_x)
    done = r_o.third()
    r_in.ra = after(r_in.ra, done)
    done = r_in.second()
    vec_out = lax.optimization_barrier(vec_grad).reshape(nvec, size, vcols).transpose(1, 0, 2).reshape(size, nvec * vcols)
    vec_high = lax.optimization_barrier(vec_out.astype(bf))
    vec_low = (vec_out - vec_high.astype(f32)).astype(bf)
    vec_out = jnp.pad(
        jnp.concatenate([vec_high, vec_low], axis=1),
        ((0, 0), (0, 16 * bcols - 2 * nvec * vcols)),
    ).reshape(size, 16, bcols)
    r_in.ra, vec_out, r_o.parts = after((r_in.ra, vec_out, r_o.parts), done)
    done = r_in.third()
    s_o = r_o.last()
    r_in.parts = after(r_in.parts, s_o)
    s_in = r_in.last()

    mine = jnp.concatenate([s_in, s_o, s_cq, s_ckv, s_co, s_up, s_dt], axis=1)
    blocks = jnp.take(mine.reshape(rp, nblk, bcols).transpose(1, 0, 2), slot_block, axis=0)
    blocks = jnp.concatenate([blocks.reshape(size, per_dev * rp, bcols), vec_out], axis=1)
    got = lax.all_to_all(blocks, AXES, 0, 0, tiled=True)
    vec_in = got[:, per_dev * rp :].reshape(size, 16 * bcols)[:, : 2 * nvec * vcols].astype(f32)
    share_vec = jnp.sum(vec_in.reshape(size, 2, nvec, vcols), axis=(0, 1))
    grads = (
        got[:, : per_dev * rp]
        .reshape(low, HI, per_dev, rp, bcols)
        .transpose(2, 1, 0, 3, 4)
        .reshape(per_dev, width, bcols)
    )
    my_blocks = lax.dynamic_slice(slot_block, (me * per_dev,), (per_dev,))
    bounds = jnp.array([width * j for j in range(1, 9)] + [8 * width + hidden], jnp.int32)
    which = jnp.sum((my_blocks[:, None] * bcols >= bounds[None, :]).astype(jnp.int32), axis=1)
    first_new, second_new, master_new = update(
        which, bases, grads, first_moment, second_moment, master_weights
    )
    corr_one = 1.0 - beta_one**STEP
    corr_two = 1.0 - beta_two**STEP
    vf_new = beta_one * vector_first + (1.0 - beta_one) * share_vec
    vs_new = beta_two * vector_second + (1.0 - beta_two) * share_vec * share_vec
    vec_new = vector_params - rate_vec * (vf_new / corr_one) / (
        jnp.sqrt(vs_new / corr_two) + adam_eps
    )
    return (
        out.astype(bf).reshape(hidden_in.shape),
        d_x.reshape(hidden_in.shape),
        encoder_grad.reshape(encoder_states.shape),
        first_new,
        second_new,
        master_new,
        vf_new,
        vs_new,
        vec_new,
        share_vec,
    )


def solution(mesh):
    spread_rows = P(None, ("dp", "fsdp"), None, None)
    spread_cols = P(None, ("dp", "fsdp"))
    in_specs = (
        spread_rows,
        spread_rows,
        P(None, ("dp", "fsdp"), None),
        spread_rows,
        P(("dp", "fsdp"), None, None),
        spread_cols,
        spread_cols,
        spread_cols,
        P(),
        P(),
        spread_cols,
        spread_cols,
        spread_cols,
    )
    out_specs = (spread_rows, spread_rows, P(("dp", "fsdp"), None, None)) + (spread_cols,) * 7
    return jax.shard_map(shards, mesh=mesh, in_specs=in_specs, out_specs=out_specs, check_vma=False)
```
